512 devices in a mesh: seq: 32 (over y, x), head: 16 (over z, core).
Axes of the slice: x: 4, y: 8, z: 8, core: 2. Of those that a mesh axis runs over, the one named last changes fastest.
Arguments:
- queries: bfloat16 [8192, 2048], P('seq', 'head'), may hold values from -192 to 192
- keys: bfloat16 [8192, 2048], P('seq', 'head'), may hold values from -6 to 6
- values: bfloat16 [8192, 2048], P('seq', 'head'), may hold values from -6 to 6
- out_weight: bfloat16 [2048, 3072], P('head'), may hold values from -0.125 to 0.125
- grad_mixed: bfloat16 [8192, 3072], P('seq', 'head'), may hold values from -6 to 6
- kv_tiles: int32 [128, 8], replicated, may hold values from 0 to 127, as said below
- kv_counts: int32 [128], replicated, may hold values from 1 to 8, as said below
Outputs:
- mixed: bfloat16 [8192, 3072], P('seq', 'head')
- grad_queries: bfloat16 [8192, 2048], P('seq', 'head')
- grad_keys: bfloat16 [8192, 2048], P('seq', 'head')
- grad_values: bfloat16 [8192, 2048], P('seq', 'head')
- weight_grad: bfloat16 [2048, 3072], P('head')
The draws below stay inside these ranges and needn't reach their ends.
Inputs may be any that keep to these rules, and one draw needn't show every extreme that they name: `kv_tiles`: row t lists key tiles for query tile t; the 8 entries of a row are distinct. Tile k belongs to index k // 4 of seq. Over the 4 rows i * 4 to (i + 1) * 4 - 1, all entries taken together, used or not, name the tiles of each index of seq exactly 1 times. Entries j < kv_counts[t] of row t are used.
All inputs are finite; a program needn't handle non-finite values.
Results may differ from the reference program's by a relative error of at most 0.034.
Values may be sent and summed in bfloat16 or wider, within the bound.
No kernel may reach another device: no remote copies, remote signals or barrier semaphores. Data moves between devices by JAX's collectives and lax.ppermute only.
A program may use at most 64 MiB of HBM per device.

```python
import math
import jax
import jax.numpy as jnp
from jax import lax

TILE = 64
HD = 64
HEADS_DEV = 2
D = 3072
MAXKV = 8
TILES_DEV = 4
TOKENS = 8192
HEADS = 32
N_SEQ = 32
N_HEAD = 16


def tile_lists(key):
    key = jax.random.fold_in(key, 901)
    per_owner = TILES_DEV * MAXKV // N_SEQ

    def one_device(device):
        device_key = jax.random.fold_in(key, device)
        key_order, key_base, key_low, key_counts = jax.random.split(device_key, 4)
        other_offsets = jnp.repeat(jnp.arange(1, N_SEQ, dtype=jnp.int32), per_owner)
        other_offsets = jax.random.permutation(key_order, other_offsets)
        offsets = jnp.concatenate([jnp.zeros((per_owner,), jnp.int32), other_offsets])
        owner_of = ((device + offsets) % N_SEQ).reshape(TILES_DEV, MAXKV)
        positions = jnp.arange(MAXKV, dtype=jnp.int32)
        same_owner = owner_of[:, :, None] == owner_of[:, None, :]
        earlier = positions[None, None, :] < positions[None, :, None]
        rank_in_owner = jnp.sum((same_owner & earlier).astype(jnp.int32), axis=2)
        base_tiles = jax.random.randint(key_base, (TILES_DEV, N_SEQ), 0, TILES_DEV)
        first_tile = jnp.take_along_axis(base_tiles, owner_of, axis=1)
        local_tile = (first_tile + rank_in_owner) % TILES_DEV
        lists = owner_of * TILES_DEV + local_tile
        lowest = jax.random.randint(key_low, (), 1, MAXKV + 1)
        counts = jax.random.randint(key_counts, (TILES_DEV,), lowest, MAXKV + 1)
        filled = jnp.arange(TILES_DEV, dtype=jnp.int32) * MAXKV < per_owner
        counts = jnp.where(filled, MAXKV, counts)
        return (lists.astype(jnp.int32), counts.astype(jnp.int32))
    lists, counts = jax.vmap(one_device)(jnp.arange(N_SEQ, dtype=jnp.int32))
    return (lists.reshape(N_SEQ * TILES_DEV, MAXKV), counts.reshape(N_SEQ * TILES_DEV))


def shared_keys(key):
    key = jax.random.fold_in(key, 902)
    return jax.random.normal(key, (N_SEQ * TILES_DEV * TILE, HEADS_DEV * N_HEAD * HD), jnp.float32)


def draw_keys(key, part):
    source = shared_keys(key)
    return jnp.clip(source, -6.0, 6.0).astype(jnp.bfloat16)


def draw_queries(key, part):
    source = shared_keys(key)
    key = jax.random.fold_in(key, 5)
    drawn = jnp.clip(jax.random.normal(key, source.shape, jnp.float32), -6.0, 6.0)
    return drawn.astype(jnp.bfloat16)


def draw_kv_tiles(key, part):
    lists, counts = tile_lists(key)
    return lists


def draw_kv_counts(key, part):
    lists, counts = tile_lists(key)
    return counts


def shard_levels(stream_key, extent, shards, low, top_value):
    level, own = 1.0, jax.random.fold_in(stream_key, 6)
    for position, parts in shards:
        steps = jnp.exp(jax.random.uniform(jax.random.fold_in(own, position), (parts,), jnp.float32, low / len(shards), top_value / len(shards)))
        level = level * jnp.repeat(steps, extent[position] // parts).reshape([-1 if axis == position else 1 for axis in range(len(extent))])
    return level


def normal_values(own_key, shape, spread, most, pieces=(), kind=jnp.bfloat16):
    level = shard_levels(own_key, shape, pieces, -0.22, 0.18) if pieces else 1.0
    entries = jax.random.normal(own_key, shape, jnp.float32) * spread * level
    return jnp.minimum(jnp.maximum(entries, -most), most).astype(kind)


def setup_inputs(seed: int = 0) -> dict:
    streams_of = jax.random.split(jax.random.key(seed), 8)
    return {
        "queries": draw_queries(jax.random.fold_in(streams_of[7], 71), 0),
        "keys": draw_keys(jax.random.fold_in(streams_of[7], 71), 0),
        "values": normal_values(streams_of[2], (TOKENS, HEADS * HD), 1.0, 6.0, ((0, 32), (1, 16))),
        "out_weight": normal_values(streams_of[3], (HEADS * HD, D), (HEADS * HD) ** -0.5, 0.125, ((0, 16),)),
        "grad_mixed": normal_values(streams_of[4], (TOKENS, D), 1.0, 6.0, ((0, 32), (1, 16))),
        "kv_tiles": draw_kv_tiles(jax.random.fold_in(streams_of[7], 71), 0),
        "kv_counts": draw_kv_counts(jax.random.fold_in(streams_of[7], 71), 0),
    }


def reference(queries, keys, values, out_weight, grad_mixed, kv_tiles, kv_counts):
    row_width = HEADS * HD
    score_scale = 1.0 / math.sqrt(HD)
    tile_count = kv_tiles.shape[0]
    query_tiles = queries.reshape(tile_count, TILE, HEADS, HD)
    key_tiles = keys.reshape(tile_count, TILE, HEADS, HD)
    value_tiles = values.reshape(tile_count, TILE, HEADS, HD)
    slot_numbers = jnp.arange(MAXKV, dtype=jnp.int32)

    def listed(index):
        tile_ids = kv_tiles[index]
        is_kept = jnp.repeat(slot_numbers < kv_counts[index], TILE)
        query_rows = query_tiles[index].astype(jnp.float32)
        key_rows = key_tiles[tile_ids].reshape(MAXKV * TILE, HEADS, HD).astype(jnp.float32)
        value_rows = value_tiles[tile_ids].reshape(MAXKV * TILE, HEADS, HD).astype(jnp.float32)
        scores = jnp.einsum('qhd,khd->hqk', query_rows, key_rows) * score_scale
        scores = jnp.where(is_kept[None, None, :], scores, -jnp.inf)
        return (tile_ids, query_rows, key_rows, value_rows, scores)

    def forward_tile(index):
        tile_ids, query_rows, key_rows, value_rows, scores = listed(index)
        row_max = lax.optimization_barrier(jnp.max(scores, axis=-1, keepdims=True))
        log_total = row_max + jnp.log(lax.optimization_barrier(jnp.sum(jnp.exp(scores - row_max), axis=-1, keepdims=True)))
        weights = lax.optimization_barrier(jnp.exp(scores - log_total).astype(jnp.bfloat16))
        attended = jnp.einsum('hqk,khd->qhd', weights.astype(jnp.float32), value_rows)
        return (attended.astype(jnp.bfloat16), log_total[..., 0])
    attention, log_totals = lax.map(forward_tile, jnp.arange(tile_count, dtype=jnp.int32))
    flat_attention = attention.reshape(tile_count * TILE, row_width)
    block_width = HEADS_DEV * HD

    def add_block(summed, block_index):
        rows = lax.dynamic_slice_in_dim(flat_attention, block_index * block_width, block_width, 1)
        weight_rows = lax.dynamic_slice_in_dim(out_weight, block_index * block_width, block_width, 0)
        partial_block = jnp.dot(rows, weight_rows, preferred_element_type=jnp.float32).astype(jnp.bfloat16)
        partial_block = lax.optimization_barrier(partial_block)
        return (summed + partial_block.astype(jnp.float32), None)
    summed, _ = lax.scan(add_block, jnp.zeros((tile_count * TILE, D), jnp.float32), jnp.arange(N_HEAD, dtype=jnp.int32))
    mixed = summed.astype(jnp.bfloat16)
    grad_attention = jnp.dot(grad_mixed, out_weight.T, preferred_element_type=jnp.float32).astype(jnp.bfloat16)
    weight_grad = jnp.dot(flat_attention.T, grad_mixed, preferred_element_type=jnp.float32).astype(jnp.bfloat16)
    grad_tiles = grad_attention.reshape(tile_count, TILE, HEADS, HD)
    row_delta = lax.optimization_barrier(jnp.sum(grad_tiles.astype(jnp.float32) * attention.astype(jnp.float32), axis=-1))

    def backward_tile(carried, index):
        key_acc, value_acc = carried
        tile_ids, query_rows, key_rows, value_rows, scores = listed(index)
        probs = jnp.exp(scores - log_totals[index][..., None])
        weights = lax.optimization_barrier(probs.astype(jnp.bfloat16)).astype(jnp.float32)
        grad_rows = grad_tiles[index].astype(jnp.float32)
        grad_probs = jnp.einsum('qhd,khd->hqk', grad_rows, value_rows)
        grad_scores = (probs * (grad_probs - row_delta[index].T[..., None])).astype(jnp.bfloat16)
        grad_scores = lax.optimization_barrier(grad_scores).astype(jnp.float32)
        grad_query = jnp.einsum('hqk,khd->qhd', grad_scores, key_rows) * score_scale
        grad_key = jnp.einsum('hqk,qhd->khd', grad_scores, query_rows) * score_scale
        grad_value = jnp.einsum('hqk,qhd->khd', weights, grad_rows)
        key_acc = key_acc.at[tile_ids].add(grad_key.reshape(MAXKV, TILE, HEADS, HD))
        value_acc = value_acc.at[tile_ids].add(grad_value.reshape(MAXKV, TILE, HEADS, HD))
        return ((key_acc, value_acc), grad_query.astype(jnp.bfloat16))
    zero_grads = jnp.zeros((tile_count, TILE, HEADS, HD), jnp.float32)
    (key_acc, value_acc), grad_queries = lax.scan(backward_tile, (zero_grads, zero_grads), jnp.arange(tile_count, dtype=jnp.int32))
    grad_queries = grad_queries.reshape(tile_count * TILE, row_width)
    grad_keys = key_acc.astype(jnp.bfloat16).reshape(tile_count * TILE, row_width)
    grad_values = value_acc.astype(jnp.bfloat16).reshape(tile_count * TILE, row_width)
    return (mixed, grad_queries, grad_keys, grad_values, weight_grad)
```

```python
import functools
import math

import jax
import jax.numpy as jnp
from jax import lax
from jax.experimental import pallas as pl
from jax.experimental.pallas import tpu as pltpu
from jax.sharding import PartitionSpec as P

TILE = 64
HD = 64
WIDTH = 2 * HD
STAT_ROWS = 16
BF16 = jnp.bfloat16
F32 = jnp.float32
VMEM = pl.BlockSpec(memory_space=pltpu.VMEM)
SMEM = pl.BlockSpec(memory_space=pltpu.SMEM)
PARAMS = pltpu.CompilerParams(vmem_limit_bytes=32 * 1024 * 1024)
NT = (((1,), (1,)), ((), ()))


def dot(a, b):
    return jnp.dot(a, b, preferred_element_type=F32)


def dot_nt(a, b):
    return lax.dot_general(a, b, NT, preferred_element_type=F32)


def split_heads(rows):
    lane = lax.broadcasted_iota(jnp.int32, rows.shape, 1)
    zero = jnp.zeros_like(rows)
    return jnp.concatenate(
        [jnp.where(lane < HD, rows, zero), jnp.where(lane < HD, zero, rows)], axis=0
    )


def join_heads(rows):
    half = rows.shape[0] // 2
    lane = lax.broadcasted_iota(jnp.int32, (half, rows.shape[1]), 1)
    return jnp.where(lane < HD, rows[:half], rows[half:])


def tables(kv_tiles, kv_counts, seq_count, tiles_dev, device):
    list_length = kv_tiles.shape[1]
    entries = tiles_dev * list_length
    lists = kv_tiles.reshape(seq_count, entries)
    owner = lists // tiles_dev
    position = jnp.arange(entries, dtype=jnp.int32)
    kept = (position % list_length)[None, :] < jnp.repeat(
        kv_counts.reshape(seq_count, tiles_dev), list_length, axis=1
    )
    here = owner == device
    tile_asked = jnp.sum(jnp.where(here, lists % tiles_dev, 0), axis=1)
    used = jnp.sum(jnp.where(here & kept, 1, 0), axis=1)
    own = lax.dynamic_slice_in_dim(owner, device, 1, 0)[0]
    owners = jnp.arange(seq_count, dtype=jnp.int32)
    query_tile = jnp.sum(
        jnp.where(own[None, :] == owners[:, None], position[None, :] // list_length, 0), axis=1
    )
    counts = lax.dynamic_slice_in_dim(kv_counts, device * tiles_dev, tiles_dev, 0)
    counts = jnp.pad(counts, (0, entries - tiles_dev))
    return jnp.stack([tile_asked, used, own, query_tile, counts])


def pack_kernel(table, queries, keys, values, out):
    def step(i, carry):
        tile = pl.ds(pl.multiple_of(table[0, i] * TILE, TILE), TILE)
        out[i, 0:TILE, :] = keys[tile, :]
        out[i, TILE : 2 * TILE, :] = values[tile, :]
        mine = pl.ds(pl.multiple_of(table[3, i] * TILE, TILE), TILE)
        out[i, 2 * TILE : 3 * TILE, :] = queries[mine, :]
        return carry

    lax.fori_loop(0, out.shape[0], step, 0)


def listed(table, fetched, tile, list_length, part):
    return jnp.concatenate(
        [
            fetched[table[2, tile * list_length + j], part * TILE : (part + 1) * TILE, :]
            for j in range(list_length)
        ],
        axis=0,
    )


def tile_scores(table, query2, key_rows, tile, scale):
    scores = dot_nt(query2, key_rows) * scale
    column = lax.broadcasted_iota(jnp.int32, scores.shape, 1)
    return jnp.where(column < table[4, tile] * TILE, scores, -jnp.inf)


def forward_kernel(
    scale, list_length, table, fetched, queries, grad_t, weight, out, attention, grads, stats, spread
):
    tiles = queries.shape[0] // TILE
    seq_count = out.shape[0]
    chunk = grad_t.shape[0] // seq_count
    grads[...] = dot(weight[...], grad_t[...]).T.astype(BF16)
    lane = lax.broadcasted_iota(jnp.int32, (WIDTH, WIDTH), 1)
    table_of_stats = jnp.zeros((WIDTH, WIDTH), F32)
    for tile in range(tiles):
        rows = slice(tile * TILE, (tile + 1) * TILE)
        query2 = split_heads(queries[rows, :])
        key_rows = listed(table, fetched, tile, list_length, 0)
        value_rows = listed(table, fetched, tile, list_length, 1)
        scores = tile_scores(table, query2, key_rows, tile, scale)
        top = jnp.max(scores, axis=1, keepdims=True)
        log_total = top + jnp.log(jnp.sum(jnp.exp(scores - top), axis=1, keepdims=True))
        weights = jnp.exp(scores - log_total).astype(BF16)
        attended = join_heads(dot(weights, value_rows)).astype(BF16)
        attention[rows, :] = attended
        product = grads[rows, :].astype(F32) * attended.astype(F32)
        delta = jnp.sum(split_heads(product), axis=1, keepdims=True)
        table_of_stats = jnp.where(lane == tile, log_total, table_of_stats)
        table_of_stats = jnp.where(lane == tiles + tile, delta, table_of_stats)
    stats[...] = table_of_stats
    by_row = table_of_stats.T
    row = lax.broadcasted_iota(jnp.int32, (STAT_ROWS, WIDTH), 0)
    for tile in range(tiles):
        block = jnp.zeros((STAT_ROWS, WIDTH), F32)
        for at, value in ((0, by_row[tile : tile + 1]), (3, by_row[tiles + tile : tiles + tile + 1])):
            for part in range(3):
                rounded = value.astype(BF16).astype(F32)
                block = jnp.where(row == at + part, rounded, block)
                value = value - rounded
        spread[tile, 0:TILE, :] = grads[tile * TILE : (tile + 1) * TILE, :]
        spread[tile, TILE : TILE + STAT_ROWS, :] = block.astype(BF16)

    def step(i, carry):
        start = pl.multiple_of(i * chunk, chunk)
        part = dot(grad_t[pl.ds(start, chunk), :], attention[...])
        out[i, 0:chunk, :] = part.astype(BF16)
        out[i, chunk : chunk + TILE + STAT_ROWS, :] = spread[table[3, i]]
        return carry

    lax.fori_loop(0, seq_count, step, 0, unroll=4)


def query_kernel(scale, list_length, table, fetched, queries, grads, stats, out):
    tiles = queries.shape[0] // TILE
    for tile in range(tiles):
        rows = slice(tile * TILE, (tile + 1) * TILE)
        key_rows = listed(table, fetched, tile, list_length, 0)
        value_rows = listed(table, fetched, tile, list_length, 1)
        scores = tile_scores(table, split_heads(queries[rows, :]), key_rows, tile, scale)
        probs = jnp.exp(scores - stats[:, tile : tile + 1])
        grad_probs = dot_nt(split_heads(grads[rows, :]), value_rows)
        grad_scores = (probs * (grad_probs - stats[:, tiles + tile : tiles + tile + 1])).astype(BF16)
        out[rows, :] = (join_heads(dot(grad_scores, key_rows)) * scale).astype(BF16)


def sum_kernel(chunk, arrived, out):
    total = arrived[0, 0:chunk, :].astype(F32)
    for i in range(1, arrived.shape[0]):
        total += arrived[i, 0:chunk, :].astype(F32)
    total = total.astype(BF16)
    for i in range(out.shape[0]):
        out[i] = total


def owner_kernel(scale, chunk, group, table, fetched, arrived, keys, values, grad_keys, grad_values, key_sum, value_sum):
    tok_rows = keys.shape[0]
    senders = arrived.shape[0]
    key_tile = lax.broadcasted_iota(jnp.int32, (tok_rows, WIDTH), 0) // TILE
    key_sum[...] = jnp.zeros_like(key_sum)
    value_sum[...] = jnp.zeros_like(value_sum)

    def step(at, carry):
        query2, grad2, logs, deltas, keeps = [], [], [], [], []
        for k in range(group):
            i = at * group + k
            query2.append(split_heads(fetched[i, 2 * TILE : 3 * TILE, :]))
            grad2.append(split_heads(arrived[i, chunk : chunk + TILE, :]))
            parts = arrived[i, chunk + TILE : chunk + TILE + STAT_ROWS, :].astype(F32)
            logs.append(parts[0:1] + parts[1:2] + parts[2:3])
            deltas.append(parts[3:4] + parts[4:5] + parts[5:6])
            wanted = jnp.where(table[1, i] > 0, table[0, i], -1)
            keeps.append(key_tile == wanted)
        query2 = jnp.concatenate(query2, axis=0)
        grad2 = jnp.concatenate(grad2, axis=0)
        log_total = jnp.concatenate(logs, axis=1)
        delta = jnp.concatenate(deltas, axis=1)
        scores = dot_nt(keys[...], query2) * scale
        gaps = scores - log_total
        gaps = jnp.concatenate(
            [
                jnp.where(keeps[k], gaps[:, k * WIDTH : (k + 1) * WIDTH], -jnp.inf)
                for k in range(group)
            ],
            axis=1,
        )
        probs = jnp.exp(gaps)
        grad_probs = dot_nt(values[...], grad2)
        grad_scores = (probs * (grad_probs - delta)).astype(BF16)
        key_sum[...] += dot(grad_scores, query2)
        value_sum[...] += dot(probs.astype(BF16), grad2)
        return carry

    lax.fori_loop(0, senders // group, step, 0)
    grad_keys[...] = (key_sum[...] * scale).astype(BF16)
    grad_values[...] = value_sum[...].astype(BF16)


def exchange(blocks):
    return lax.all_to_all(blocks, "seq", split_axis=0, concat_axis=0, tiled=True)


def body(queries, keys, values, out_weight, grad_mixed, kv_tiles, kv_counts):
    tok_rows, row_width = queries.shape
    tiles_dev = tok_rows // TILE
    list_length = kv_tiles.shape[1]
    seq_count = lax.axis_size("seq")
    scale = 1.0 / math.sqrt(HD)
    model = out_weight.shape[1]
    chunk = model // seq_count
    device = lax.axis_index("seq")
    block = jax.ShapeDtypeStruct((tok_rows, row_width), BF16)

    table = tables(kv_tiles, kv_counts, seq_count, tiles_dev, device)
    outgoing = pl.pallas_call(
        pack_kernel,
        out_shape=jax.ShapeDtypeStruct((seq_count, 3 * TILE, row_width), BF16),
        in_specs=[SMEM, VMEM, VMEM, VMEM],
        out_specs=VMEM,
        compiler_params=PARAMS,
        name="pack",
    )(table, queries, keys, values)
    grad_t = lax.all_gather(grad_mixed.T, "head", axis=0, tiled=True)
    fetched = exchange(outgoing)

    second, attention, grads, stats = pl.pallas_call(
        functools.partial(forward_kernel, scale, list_length),
        out_shape=(
            jax.ShapeDtypeStruct((seq_count, chunk + TILE + STAT_ROWS, row_width), BF16),
            block,
            block,
            jax.ShapeDtypeStruct((WIDTH, WIDTH), F32),
        ),
        in_specs=[SMEM, VMEM, VMEM, VMEM, VMEM],
        out_specs=(VMEM, VMEM, VMEM, VMEM),
        scratch_shapes=[pltpu.VMEM((tiles_dev, TILE + STAT_ROWS, row_width), BF16)],
        compiler_params=PARAMS,
        name="forward",
    )(table, fetched, queries, grad_t, out_weight)
    arrived = exchange(second)

    mixed_t = lax.dot_general(
        out_weight, attention, (((0,), (1,)), ((), ())), preferred_element_type=F32
    ).astype(BF16)
    mixed = lax.psum_scatter(mixed_t, "head", scatter_dimension=0, tiled=True).T

    grad_queries = pl.pallas_call(
        functools.partial(query_kernel, scale, list_length),
        out_shape=block,
        in_specs=[SMEM, VMEM, VMEM, VMEM, VMEM],
        out_specs=VMEM,
        compiler_params=PARAMS,
        cost_estimate=pl.CostEstimate(flops=400_000_000, bytes_accessed=4_000_000, transcendentals=300_000),
        name="query_grad",
    )(table, fetched, queries, grads, stats)

    third = pl.pallas_call(
        functools.partial(sum_kernel, chunk),
        out_shape=jax.ShapeDtypeStruct((seq_count, chunk, row_width), BF16),
        in_specs=[VMEM],
        out_specs=VMEM,
        compiler_params=PARAMS,
        name="sum_share",
    )(arrived)
    gathered = exchange(third)

    grad_keys, grad_values = pl.pallas_call(
        functools.partial(owner_kernel, scale, chunk, 4),
        out_shape=(block, block),
        in_specs=[SMEM, VMEM, VMEM, VMEM, VMEM],
        out_specs=(VMEM, VMEM),
        scratch_shapes=[pltpu.VMEM((tok_rows, row_width), F32), pltpu.VMEM((tok_rows, row_width), F32)],
        compiler_params=PARAMS,
        cost_estimate=pl.CostEstimate(flops=1_100_000_000, bytes_accessed=4_000_000, transcendentals=1_000_000),
        name="owner_grad",
    )(table, fetched, arrived, keys, values)
    weight_grad = gathered.reshape(model, row_width).T
    return (mixed, grad_queries, grad_keys, grad_values, weight_grad)


def solution(mesh):
    return jax.shard_map(
        body,
        mesh=mesh,
        in_specs=(
            P("seq", "head"),
            P("seq", "head"),
            P("seq", "head"),
            P("head", None),
            P("seq", "head"),
            P(),
            P(),
        ),
        out_specs=(
            P("seq", "head"),
            P("seq", "head"),
            P("seq", "head"),
            P("seq", "head"),
            P("head", None),
        ),
        check_vma=False,
    )
```

```python
import functools
import math

import jax
import jax.numpy as jnp
from jax import lax
from jax.experimental import pallas as pl
from jax.experimental.pallas import tpu as pltpu
from jax.sharding import Mesh, PartitionSpec as P

TILE = 64
HD = 64
WIDTH = 2 * HD
STAT_ROWS = 8
ROW_BLOCKS = 4
COL_BLOCKS = 8
BF16 = jnp.bfloat16
F32 = jnp.float32
VMEM = pl.BlockSpec(memory_space=pltpu.VMEM)
SMEM = pl.BlockSpec(memory_space=pltpu.SMEM)
HBM = pl.BlockSpec(memory_space=pltpu.HBM)
PARAMS = pltpu.CompilerParams(vmem_limit_bytes=32 * 1024 * 1024)
NT = (((1,), (1,)), ((), ()))


def stay(array):
    return pltpu.with_memory_space_constraint(array, pltpu.HBM)


def dot(a, b):
    return jnp.dot(a, b, preferred_element_type=F32)


def dot_nt(a, b):
    return lax.dot_general(a, b, NT, preferred_element_type=F32)


def split_heads(rows):
    lane = lax.broadcasted_iota(jnp.int32, rows.shape, 1)
    zero = jnp.zeros_like(rows)
    return jnp.concatenate(
        [jnp.where(lane < HD, rows, zero), jnp.where(lane < HD, zero, rows)], axis=0
    )


def join_heads(rows):
    half = rows.shape[0] // 2
    lane = lax.broadcasted_iota(jnp.int32, (half, rows.shape[1]), 1)
    return jnp.where(lane < HD, rows[:half], rows[half:])


def pack_kernel(
    place, lists_h, counts_h, queries, keys, values, out, table,
    lists, counts, lists_v, counts_v, staged, codes_v, codes, held, sems,
):
    list_length, tile_count = lists_v.shape
    seq_count = out.shape[0]
    tiles = tile_count // seq_count
    device = place[0]
    pairs = (
        (lists_h, lists_v), (counts_h, counts_v), (lists_h, lists), (counts_h, counts),
        (keys, held.at[0]), (values, held.at[1]), (queries, held.at[2]),
    )
    loads = [pltpu.make_async_copy(*pair, sems.at[k]) for k, pair in enumerate(pairs)]
    for load in loads:
        load.start()
    for load in loads[:2]:
        load.wait()
    listed_tile = lists_v[...]
    entry = lax.broadcasted_iota(jnp.int32, listed_tile.shape, 0)
    code = lax.rem(listed_tile, tiles) + jnp.where(entry < counts_v[...], tiles, 0)
    code = jnp.where(lax.div(listed_tile, tiles) == device, code, 0)
    code = jnp.broadcast_to(jnp.sum(code, axis=0, keepdims=True), code.shape)
    codes_v[...] = sum(
        (pltpu.roll(code, tile_count - tile, 1) for tile in range(1, tiles)), start=code
    )
    scalars = pltpu.make_async_copy(codes_v, codes, sems.at[7])
    scalars.start()
    for load in loads[2:4]:
        load.wait()
    for tile in range(tiles):
        table[4, tile] = counts[0, device * tiles + tile]
        for j in range(list_length):
            owner = lax.div(lists[j, device * tiles + tile], tiles)
            table[2, tile * list_length + j] = owner
            table[3, owner] = tile
    scalars.wait()
    for load in loads[4:]:
        load.wait()
    groups = staged.shape[0]
    stores = []
    for group in range(groups):
        for k in range(seq_count // groups):
            i = group * (seq_count // groups) + k
            code = codes[0, i * tiles]
            asked = lax.rem(code, tiles)
            table[0, i] = asked
            table[1, i] = lax.div(code, tiles)
            tile = pl.ds(pl.multiple_of(asked * TILE, TILE), TILE)
            staged[group, k, 0:TILE, :] = held[0, tile, :]
            staged[group, k, TILE : 2 * TILE, :] = held[1, tile, :]
            mine = pl.ds(pl.multiple_of(table[3, i] * TILE, TILE), TILE)
            staged[group, k, 2 * TILE : 3 * TILE, :] = held[2, mine, :]
        span = pl.ds(group * (seq_count // groups), seq_count // groups)
        stores.append(pltpu.make_async_copy(staged.at[group], out.at[span], sems.at[8 + group]))
        stores[-1].start()
    for store in stores:
        store.wait()


def grad_kernel(weight_h, grad_h, grads, grad_t, weight, sems):
    runs = sems.shape[0] - 1
    span = grad_t.shape[0] // runs
    loads = [pltpu.make_async_copy(weight_h, weight, sems.at[runs])]
    for at in range(runs):
        rows = pl.ds(at * span, span)
        loads.append(pltpu.make_async_copy(grad_h.at[rows], grad_t.at[rows], sems.at[at]))
    for load in loads:
        load.start()
    loads[0].wait()
    total = jnp.zeros((WIDTH, grads.shape[0]), F32)
    for at in range(runs):
        loads[1 + at].wait()
        rows = slice(at * span, (at + 1) * span)
        total += dot(weight[:, rows], grad_t[rows, :])
    grads[...] = total.T.astype(BF16)


def halves_kernel(run, place, weight, kept, given):
    weight_t = weight[...].T
    mine = place[0] == 0
    for z in range(kept.shape[0] // run):
        first = weight_t[2 * z * run : (2 * z + 1) * run]
        second = weight_t[(2 * z + 1) * run : (2 * z + 2) * run]
        rows = slice(z * run, (z + 1) * run)
        kept[rows, :] = jnp.where(mine, first, second)
        given[rows, :] = jnp.where(mine, second, first)


def mixed_kernel(kept, got, attention, other, out):
    step = 256
    for at in range(0, out.shape[0], step):
        rows = slice(at, at + step)
        total = dot_nt(kept[rows, :], attention[...]) + dot_nt(got[rows, :], other[...])
        out[rows, :] = total.astype(BF16)


def listed(table, fetched, tile, list_length, part):
    return jnp.concatenate(
        [
            fetched[table[2, tile * list_length + j], part * TILE : (part + 1) * TILE, :]
            for j in range(list_length)
        ],
        axis=0,
    )


def tile_scores(table, query2, key_rows, tile, scale):
    scores = dot_nt(query2, key_rows) * scale
    column = lax.broadcasted_iota(jnp.int32, scores.shape, 1)
    return jnp.where(column < table[4, tile] * TILE, scores, -jnp.inf)


def forward_kernel(
    scale, list_length, table, fetched, queries, grad_t, grads, out, attention, stats,
    spread, staged, sems,
):
    tiles = queries.shape[0] // TILE
    seq_count = out.shape[0]
    model = grad_t.shape[0]
    chunk = model // seq_count
    wide = model // COL_BLOCKS
    tall = WIDTH // ROW_BLOCKS
    lane = lax.broadcasted_iota(jnp.int32, (WIDTH, WIDTH), 1)
    table_of_stats = jnp.zeros((WIDTH, WIDTH), F32)
    for tile in range(tiles):
        rows = slice(tile * TILE, (tile + 1) * TILE)
        query2 = split_heads(queries[rows, :])
        key_rows = listed(table, fetched, tile, list_length, 0)
        value_rows = listed(table, fetched, tile, list_length, 1)
        scores = tile_scores(table, query2, key_rows, tile, scale)
        top = jnp.max(scores, axis=1, keepdims=True)
        log_total = top + jnp.log(jnp.sum(jnp.exp(scores - top), axis=1, keepdims=True))
        weights = jnp.exp(scores - log_total).astype(BF16)
        attended = join_heads(dot(weights, value_rows)).astype(BF16)
        attention[rows, :] = attended
        product = grads[rows, :].astype(F32) * attended.astype(F32)
        delta = jnp.sum(split_heads(product), axis=1, keepdims=True)
        table_of_stats = jnp.where(lane == tile, log_total, table_of_stats)
        table_of_stats = jnp.where(lane == tiles + tile, delta, table_of_stats)
    stats[...] = table_of_stats
    by_row = table_of_stats.T
    row = lax.broadcasted_iota(jnp.int32, (STAT_ROWS, WIDTH), 0)
    for tile in range(tiles):
        block = jnp.zeros((STAT_ROWS, WIDTH), F32)
        for at, value in ((0, by_row[tile : tile + 1]), (3, by_row[tiles + tile : tiles + tile + 1])):
            for part in range(3):
                rounded = value.astype(BF16).astype(F32)
                block = jnp.where(row == at + part, rounded, block)
                value = value - rounded
        spread[tile, 0:TILE, :] = grads[tile * TILE : (tile + 1) * TILE, :]
        spread[tile, TILE : TILE + STAT_ROWS, :] = block.astype(BF16)

    for i in range(seq_count):
        staged[i, chunk : chunk + TILE + STAT_ROWS, :] = spread[table[3, i]]
    attention_t = attention[...].astype(F32).T.astype(BF16)
    stores = []
    for at in range(COL_BLOCKS):
        part = dot_nt(attention_t, grad_t[at * wide : (at + 1) * wide, :]).astype(BF16)
        for down in range(ROW_BLOCKS):
            for k in range(wide // WIDTH):
                staged[at * ROW_BLOCKS + down, k * tall : (k + 1) * tall, :] = part[
                    down * tall : (down + 1) * tall, k * WIDTH : (k + 1) * WIDTH
                ]
        if at % 2 == 1:
            span = pl.ds((at - 1) * ROW_BLOCKS, 2 * ROW_BLOCKS)
            stores.append(pltpu.make_async_copy(staged.at[span], out.at[span], sems.at[at // 2]))
            stores[-1].start()
    for store in stores:
        store.wait()


def query_kernel(scale, list_length, table, fetched, queries, grads, stats, out):
    tiles = queries.shape[0] // TILE
    for tile in range(tiles):
        rows = slice(tile * TILE, (tile + 1) * TILE)
        key_rows = listed(table, fetched, tile, list_length, 0)
        value_rows = listed(table, fetched, tile, list_length, 1)
        scores = tile_scores(table, split_heads(queries[rows, :]), key_rows, tile, scale)
        probs = jnp.exp(scores - stats[:, tile : tile + 1])
        grad_probs = dot_nt(split_heads(grads[rows, :]), value_rows)
        grad_scores = (probs * (grad_probs - stats[:, tiles + tile : tiles + tile + 1])).astype(BF16)
        out[rows, :] = (join_heads(dot(grad_scores, key_rows)) * scale).astype(BF16)


def sum_kernel(chunk, arrived, out, total_of, sems):
    total = arrived[0, 0:chunk, :].astype(F32)
    for i in range(1, arrived.shape[0]):
        total += arrived[i, 0:chunk, :].astype(F32)
    total = total.astype(BF16)
    copies = total_of.shape[0]
    for i in range(copies):
        total_of[i] = total
    stores = []
    for at in range(out.shape[0] // copies):
        stores.append(pltpu.make_async_copy(total_of, out.at[pl.ds(at * copies, copies)], sems.at[at]))
        stores[-1].start()
    for store in stores:
        store.wait()


def owner_kernel(scale, chunk, group, table, fetched, arrived, keys, values, grad_keys, grad_values, key_sum, value_sum):
    tok_rows = keys.shape[0]
    senders = arrived.shape[0]
    key_tile = lax.broadcasted_iota(jnp.int32, (tok_rows, WIDTH), 0) // TILE
    key_sum[...] = jnp.zeros_like(key_sum)
    value_sum[...] = jnp.zeros_like(value_sum)

    def step(at, carry):
        query2, grad2, logs, deltas, keeps = [], [], [], [], []
        for k in range(group):
            i = at * group + k
            query2.append(split_heads(fetched[i, 2 * TILE : 3 * TILE, :]))
            grad2.append(split_heads(arrived[i, chunk : chunk + TILE, :]))
            parts = arrived[i, chunk + TILE : chunk + TILE + STAT_ROWS, :].astype(F32)
            logs.append(parts[0:1] + parts[1:2] + parts[2:3])
            deltas.append(parts[3:4] + parts[4:5] + parts[5:6])
            wanted = jnp.where(table[1, i] > 0, table[0, i], -1)
            keeps.append(key_tile == wanted)
        query2 = jnp.concatenate(query2, axis=0)
        grad2 = jnp.concatenate(grad2, axis=0)
        log_total = jnp.concatenate(logs, axis=1)
        delta = jnp.concatenate(deltas, axis=1)
        scores = dot_nt(keys[...], query2) * scale
        gaps = scores - log_total
        gaps = jnp.concatenate(
            [
                jnp.where(keeps[k], gaps[:, k * WIDTH : (k + 1) * WIDTH], -jnp.inf)
                for k in range(group)
            ],
            axis=1,
        )
        probs = jnp.exp(gaps)
        grad_probs = dot_nt(values[...], grad2)
        grad_scores = (probs * (grad_probs - delta)).astype(BF16)
        key_sum[...] += dot(grad_scores, query2)
        value_sum[...] += dot(probs.astype(BF16), grad2)
        return carry

    lax.fori_loop(0, senders // group, step, 0)
    grad_keys[...] = (key_sum[...] * scale).astype(BF16)
    grad_values[...] = value_sum[...].astype(BF16)


def assemble_kernel(gathered, out, held, staged, sems):
    tall = out.shape[0] // ROW_BLOCKS
    wide = out.shape[1] // COL_BLOCKS
    loads, stores = [], []
    for at in range(COL_BLOCKS):
        span = pl.ds(at * ROW_BLOCKS, ROW_BLOCKS)
        loads.append(pltpu.make_async_copy(gathered.at[span], held.at[span], sems.at[COL_BLOCKS + at]))
        loads[-1].start()
    for at in range(COL_BLOCKS):
        loads[at].wait()
        for down in range(ROW_BLOCKS):
            for k in range(wide // WIDTH):
                column = at * wide + k * WIDTH
                staged[down * tall : (down + 1) * tall, column : column + WIDTH] = held[
                    at * ROW_BLOCKS + down, k * tall : (k + 1) * tall, :
                ]
        span = pl.ds(at * wide, wide)
        stores.append(pltpu.make_async_copy(staged.at[:, span], out.at[:, span], sems.at[at]))
        stores[-1].start()
    for store in stores:
        store.wait()


def exchange(blocks):
    return lax.all_to_all(blocks, "seq", split_axis=0, concat_axis=0, tiled=True)


def swap_cores(array):
    return lax.ppermute(array, "core", [(0, 1), (1, 0)])


def body(queries, keys, values, out_weight, grad_mixed, kv_tiles, kv_counts):
    tok_rows, row_width = queries.shape
    tiles_dev = tok_rows // TILE
    list_length = kv_tiles.shape[1]
    seq_count = lax.axis_size("seq")
    scale = 1.0 / math.sqrt(HD)
    model = out_weight.shape[1]
    chunk = model // seq_count
    device = lax.axis_index("seq")
    block = jax.ShapeDtypeStruct((tok_rows, row_width), BF16)

    grad_t = lax.all_gather(grad_mixed.T, ("z", "core"), axis=0, tiled=True)
    lists = kv_tiles.T
    groups = 4
    outgoing, table = pl.pallas_call(
        pack_kernel,
        out_shape=(
            pltpu.HBM((seq_count, 3 * TILE, row_width), BF16),
            jax.ShapeDtypeStruct((5, seq_count), jnp.int32),
        ),
        in_specs=[SMEM, HBM, HBM, HBM, HBM, HBM],
        out_specs=(HBM, SMEM),
        scratch_shapes=[
            pltpu.SMEM(lists.shape, jnp.int32),
            pltpu.SMEM((1,) + kv_counts.shape, jnp.int32),
            pltpu.VMEM(lists.shape, jnp.int32),
            pltpu.VMEM((1,) + kv_counts.shape, jnp.int32),
            pltpu.VMEM((groups, seq_count // groups, 3 * TILE, row_width), BF16),
            pltpu.VMEM(lists.shape, jnp.int32),
            pltpu.SMEM(lists.shape, jnp.int32),
            pltpu.VMEM((3, tok_rows, row_width), BF16),
            pltpu.SemaphoreType.DMA((8 + groups,)),
        ],
        compiler_params=PARAMS,
        name="pack",
    )(
        device[None].astype(jnp.int32),
        stay(lists),
        stay(kv_counts[None, :]),
        stay(queries),
        stay(keys),
        stay(values),
    )
    fetched = exchange(outgoing)
    half = jax.ShapeDtypeStruct((model // 2, row_width), BF16)
    kept, given = pl.pallas_call(
        functools.partial(halves_kernel, grad_mixed.shape[1]),
        out_shape=(half, half),
        in_specs=[SMEM, VMEM],
        out_specs=(VMEM, VMEM),
        compiler_params=PARAMS,
        name="weight_halves",
    )(lax.axis_index("core")[None].astype(jnp.int32), out_weight)
    got = swap_cores(given)
    grads, grad_t = pl.pallas_call(
        grad_kernel,
        out_shape=(block, jax.ShapeDtypeStruct((model, tok_rows), BF16)),
        in_specs=[HBM, HBM],
        out_specs=(VMEM, VMEM),
        scratch_shapes=[
            pltpu.VMEM(out_weight.shape, BF16),
            pltpu.SemaphoreType.DMA((5,)),
        ],
        compiler_params=PARAMS,
        cost_estimate=pl.CostEstimate(flops=30_000_000_000, bytes_accessed=100_000_000, transcendentals=0),
        name="attention_grad",
    )(stay(out_weight), stay(grad_t))

    second, attention, stats = pl.pallas_call(
        functools.partial(forward_kernel, scale, list_length),
        out_shape=(
            pltpu.HBM((seq_count, chunk + TILE + STAT_ROWS, row_width), BF16),
            block,
            jax.ShapeDtypeStruct((WIDTH, WIDTH), F32),
        ),
        in_specs=[SMEM, VMEM, VMEM, VMEM, VMEM],
        out_specs=(HBM, VMEM, VMEM),
        scratch_shapes=[
            pltpu.VMEM((tiles_dev, TILE + STAT_ROWS, row_width), BF16),
            pltpu.VMEM((seq_count, chunk + TILE + STAT_ROWS, row_width), BF16),
            pltpu.SemaphoreType.DMA((COL_BLOCKS // 2,)),
        ],
        compiler_params=PARAMS,
        name="forward",
    )(table, fetched, queries, grad_t, grads)
    arrived = exchange(second)

    mixed_t = pl.pallas_call(
        mixed_kernel,
        out_shape=jax.ShapeDtypeStruct((model // 2, tok_rows), BF16),
        in_specs=[VMEM, VMEM, VMEM, VMEM],
        out_specs=VMEM,
        compiler_params=PARAMS,
        name="mixed_share",
    )(kept, got, attention, swap_cores(attention))
    mixed = lax.psum_scatter(mixed_t, "z", scatter_dimension=0, tiled=True).T

    grad_queries = pl.pallas_call(
        functools.partial(query_kernel, scale, list_length),
        out_shape=block,
        in_specs=[SMEM, VMEM, VMEM, VMEM, VMEM],
        out_specs=VMEM,
        compiler_params=PARAMS,
        cost_estimate=pl.CostEstimate(flops=400_000_000, bytes_accessed=4_000_000, transcendentals=300_000),
        name="query_grad",
    )(table, fetched, queries, grads, stats)

    third = pl.pallas_call(
        functools.partial(sum_kernel, chunk),
        out_shape=pltpu.HBM((seq_count, chunk, row_width), BF16),
        in_specs=[VMEM],
        out_specs=HBM,
        scratch_shapes=[pltpu.VMEM((4, chunk, row_width), BF16), pltpu.SemaphoreType.DMA((seq_count // 4,))],
        compiler_params=PARAMS,
        name="sum_share",
    )(arrived)
    gathered = exchange(third)

    grad_keys, grad_values = pl.pallas_call(
        functools.partial(owner_kernel, scale, chunk, 4),
        out_shape=(block, block),
        in_specs=[SMEM, VMEM, VMEM, VMEM, VMEM],
        out_specs=(VMEM, VMEM),
        scratch_shapes=[pltpu.VMEM((tok_rows, row_width), F32), pltpu.VMEM((tok_rows, row_width), F32)],
        compiler_params=PARAMS,
        cost_estimate=pl.CostEstimate(flops=1_100_000_000, bytes_accessed=4_000_000, transcendentals=1_000_000),
        name="owner_grad",
    )(table, fetched, arrived, keys, values)
    weight_grad = pl.pallas_call(
        assemble_kernel,
        out_shape=pltpu.HBM(out_weight.shape, BF16),
        in_specs=[HBM],
        out_specs=HBM,
        scratch_shapes=[
            pltpu.VMEM((seq_count, chunk, row_width), BF16),
            pltpu.VMEM(out_weight.shape, BF16),
            pltpu.SemaphoreType.DMA((2 * COL_BLOCKS,)),
        ],
        compiler_params=PARAMS,
        name="assemble",
    )(stay(gathered))
    return (mixed, grad_queries, grad_keys, grad_values, weight_grad)


def solution(mesh):
    seq_count, head_count = mesh.devices.shape
    split = Mesh(mesh.devices.reshape(seq_count, head_count // 2, 2), ("seq", "z", "core"))
    both = P("seq", ("z", "core"))
    rows = P(("z", "core"), None)
    return jax.shard_map(
        body,
        mesh=split,
        in_specs=(both, both, both, rows, both, P(), P()),
        out_specs=(both, both, both, both, rows),
        check_vma=False,
    )
```

```python
import functools
import math

import jax
import jax.numpy as jnp
from jax import lax
from jax.experimental import pallas as pl
from jax.experimental.pallas import tpu as pltpu
from jax.sharding import Mesh, PartitionSpec as P

TILE = 64
HD = 64
WIDTH = 2 * HD
STAT_ROWS = 8
ROW_BLOCKS = 4
COL_BLOCKS = 8
GATHERED = 16
NEAR = 4
BF16 = jnp.bfloat16
F32 = jnp.float32
VMEM = pl.BlockSpec(memory_space=pltpu.VMEM)
SMEM = pl.BlockSpec(memory_space=pltpu.SMEM)
HBM = pl.BlockSpec(memory_space=pltpu.HBM)
ANY = pl.BlockSpec(memory_space=pl.ANY)
PARAMS = pltpu.CompilerParams(vmem_limit_bytes=16 * 1024 * 1024)
NT = (((1,), (1,)), ((), ()))


def stay(array):
    return pltpu.with_memory_space_constraint(array, pltpu.HBM)


def dot(a, b):
    return jnp.dot(a, b, preferred_element_type=F32)


def dot_nt(a, b):
    return lax.dot_general(a, b, NT, preferred_element_type=F32)


def split_heads(rows):
    lane = lax.broadcasted_iota(jnp.int32, rows.shape, 1)
    zero = jnp.zeros_like(rows)
    return jnp.concatenate(
        [jnp.where(lane < HD, rows, zero), jnp.where(lane < HD, zero, rows)], axis=0
    )


def join_heads(rows):
    half = rows.shape[0] // 2
    lane = lax.broadcasted_iota(jnp.int32, (half, rows.shape[1]), 1)
    return jnp.where(lane < HD, rows[:half], rows[half:])


def pack_kernel(
    place, lists_h, counts_h, queries, keys, values, out, table,
    lists, counts, lists_v, counts_v, staged, codes_v, codes, held, sems,
):
    list_length, tile_count = lists_v.shape
    seq_count = out.shape[0]
    tiles = tile_count // seq_count
    device = place[0]
    pairs = (
        (lists_h, lists_v), (counts_h, counts_v), (lists_h, lists), (counts_h, counts),
        (keys, held.at[0]), (values, held.at[1]), (queries, held.at[2]),
    )
    loads = [pltpu.make_async_copy(*pair, sems.at[k]) for k, pair in enumerate(pairs)]
    for load in loads:
        load.start()
    for load in loads[:2]:
        load.wait()
    listed_tile = lists_v[...]
    entry = lax.broadcasted_iota(jnp.int32, listed_tile.shape, 0)
    code = lax.rem(listed_tile, tiles) + jnp.where(entry < counts_v[...], tiles, 0)
    code = jnp.where(lax.div(listed_tile, tiles) == device, code, 0)
    code = jnp.broadcast_to(jnp.sum(code, axis=0, keepdims=True), code.shape)
    codes_v[...] = sum(
        (pltpu.roll(code, tile_count - tile, 1) for tile in range(1, tiles)), start=code
    )
    scalars = pltpu.make_async_copy(codes_v, codes, sems.at[7])
    scalars.start()
    for load in loads[2:4]:
        load.wait()
    for tile in range(tiles):
        table[4, tile] = counts[0, device * tiles + tile]
        for j in range(list_length):
            owner = lax.div(lists[j, device * tiles + tile], tiles)
            table[2, tile * list_length + j] = owner
            table[3, owner] = tile
    scalars.wait()
    for load in loads[4:]:
        load.wait()
    groups = staged.shape[0]
    stores = []
    for group in range(groups):
        for k in range(seq_count // groups):
            i = group * (seq_count // groups) + k
            code = codes[0, i * tiles]
            asked = lax.rem(code, tiles)
            table[0, i] = asked
            table[1, i] = lax.div(code, tiles)
            tile = pl.ds(pl.multiple_of(asked * TILE, TILE), TILE)
            staged[group, k, 0:TILE, :] = held[0, tile, :]
            staged[group, k, TILE : 2 * TILE, :] = held[1, tile, :]
            mine = pl.ds(pl.multiple_of(table[3, i] * TILE, TILE), TILE)
            staged[group, k, 2 * TILE : 3 * TILE, :] = held[2, mine, :]
        span = pl.ds(group * (seq_count // groups), seq_count // groups)
        stores.append(pltpu.make_async_copy(staged.at[group], out.at[span], sems.at[8 + group]))
        stores[-1].start()
    for store in stores:
        store.wait()


def mixed_kernel(core, weight_h, attention, keep, send, weight, sem):
    load = pltpu.make_async_copy(weight_h, weight, sem)
    load.start()
    load.wait()
    chips, run = keep.shape[0], keep.shape[1]
    weight_t = weight[...].T
    first_core = core[0] == 0
    for z in range(chips):
        shares = [
            dot_nt(weight_t[(2 * z + k) * run : (2 * z + k + 1) * run], attention[...]).astype(BF16)
            for k in range(2)
        ]
        keep[z] = jnp.where(first_core, shares[0], shares[1])
        send[z] = jnp.where(first_core, shares[1], shares[0])


def pair_kernel(place, mine, arrived, keep, *sends):
    for z in range(mine.shape[0]):
        total = mine[z].astype(F32) + arrived[z].astype(F32)
        apart = jnp.bitwise_xor(place[0], z)
        slot = lax.div(apart, NEAR)
        for near, target in enumerate((keep,) + sends):

            @pl.when(lax.rem(apart, NEAR) == near)
            def _(target=target):
                target[slot] = total.astype(target.dtype)


def near_kernel(mine, *rest):
    arrived, (keep, send) = rest[:-2], rest[-2:]
    totals = []
    for i in range(2):
        total = mine[i]
        for part in arrived:
            total += part[i].astype(F32)
        totals.append(total)
    keep[...] = totals[0]
    send[...] = totals[1].astype(BF16)


def last_kernel(mine, arrived, grad_keys, out):
    out[...] = (mine[...] + arrived[...].astype(F32)).astype(BF16)


def listed(table, fetched, tile, list_length, part):
    return jnp.concatenate(
        [
            fetched[table[2, tile * list_length + j], part * TILE : (part + 1) * TILE, :]
            for j in range(list_length)
        ],
        axis=0,
    )


def tile_scores(table, query2, key_rows, tile, scale):
    scores = dot_nt(query2, key_rows) * scale
    column = lax.broadcasted_iota(jnp.int32, scores.shape, 1)
    return jnp.where(column < table[4, tile] * TILE, scores, -jnp.inf)


def forward_kernel(
    scale, list_length, table, fetched, queries, place, grad_h, other_h, weight_h, out, attention, grads, stats,
    grad_t, weight, spread, staged, sems,
):
    tiles = queries.shape[0] // TILE
    seq_count = out.shape[0]
    model = grad_t.shape[0]
    chunk = model // seq_count
    wide = model // COL_BLOCKS
    tall = WIDTH // ROW_BLOCKS
    runs = COL_BLOCKS // 2
    loads = []
    run = model // GATHERED
    core = place[0]
    for at in range(GATHERED // 2):
        span = pl.ds(at * run, run)
        first = pl.ds(pl.multiple_of((2 * at + core) * run, run), run)
        second = pl.ds(pl.multiple_of((2 * at + 1 - core) * run, run), run)
        for source, target in ((grad_h.at[span], grad_t.at[first]), (other_h.at[span], grad_t.at[second])):
            loads.append(pltpu.make_async_copy(source, target, sems.at[runs + len(loads)]))
            loads[-1].start()
    for at in range(runs):
        span = pl.ds(at * 2 * wide, 2 * wide)
        loads.append(pltpu.make_async_copy(weight_h.at[:, span], weight.at[:, span], sems.at[runs + len(loads)]))
        loads[-1].start()
    lane = lax.broadcasted_iota(jnp.int32, (WIDTH, WIDTH), 1)
    table_of_stats = jnp.zeros((WIDTH, WIDTH), F32)
    for tile in range(tiles):
        rows = slice(tile * TILE, (tile + 1) * TILE)
        query2 = split_heads(queries[rows, :])
        key_rows = listed(table, fetched, tile, list_length, 0)
        value_rows = listed(table, fetched, tile, list_length, 1)
        scores = tile_scores(table, query2, key_rows, tile, scale)
        top = jnp.max(scores, axis=1, keepdims=True)
        log_total = top + jnp.log(jnp.sum(jnp.exp(scores - top), axis=1, keepdims=True))
        weights = jnp.exp(scores - log_total).astype(BF16)
        attended = join_heads(dot(weights, value_rows)).astype(BF16)
        attention[rows, :] = attended
        table_of_stats = jnp.where(lane == tile, log_total, table_of_stats)
    grads_t = jnp.zeros((WIDTH, queries.shape[0]), F32)
    for at in range(runs):
        for load in loads[at * GATHERED // runs : (at + 1) * GATHERED // runs]:
            load.wait()
        loads[GATHERED + at].wait()
        span = slice(at * 2 * wide, (at + 1) * 2 * wide)
        grads_t += dot(weight[:, span], grad_t[span, :])
    grads[...] = grads_t.T.astype(BF16)
    for tile in range(tiles):
        rows = slice(tile * TILE, (tile + 1) * TILE)
        product = grads[rows, :].astype(F32) * attention[rows, :].astype(F32)
        delta = jnp.sum(split_heads(product), axis=1, keepdims=True)
        table_of_stats = jnp.where(lane == tiles + tile, delta, table_of_stats)
    stats[...] = table_of_stats
    by_row = table_of_stats.T
    row = lax.broadcasted_iota(jnp.int32, (STAT_ROWS, WIDTH), 0)
    for tile in range(tiles):
        block = jnp.zeros((STAT_ROWS, WIDTH), F32)
        for at, value in ((0, by_row[tile : tile + 1]), (3, by_row[tiles + tile : tiles + tile + 1])):
            for part in range(3):
                rounded = value.astype(BF16).astype(F32)
                block = jnp.where(row == at + part, rounded, block)
                value = value - rounded
        spread[tile, 0:TILE, :] = grads[tile * TILE : (tile + 1) * TILE, :]
        spread[tile, TILE : TILE + STAT_ROWS, :] = block.astype(BF16)

    for i in range(seq_count):
        staged[i, chunk : chunk + TILE + STAT_ROWS, :] = spread[table[3, i]]
    attention_t = attention[...].astype(F32).T.astype(BF16)
    stores = []
    for at in range(COL_BLOCKS):
        part = dot_nt(attention_t, grad_t[at * wide : (at + 1) * wide, :]).astype(BF16)
        for down in range(ROW_BLOCKS):
            for k in range(wide // WIDTH):
                staged[at * ROW_BLOCKS + down, k * tall : (k + 1) * tall, :] = part[
                    down * tall : (down + 1) * tall, k * WIDTH : (k + 1) * WIDTH
                ]
        if at % 2 == 1:
            span = pl.ds((at - 1) * ROW_BLOCKS, 2 * ROW_BLOCKS)
            stores.append(pltpu.make_async_copy(staged.at[span], out.at[span], sems.at[at // 2]))
            stores[-1].start()
    for store in stores:
        store.wait()


def query_kernel(scale, list_length, table, fetched, queries, grads, stats, out):
    tiles = queries.shape[0] // TILE
    for tile in range(tiles):
        rows = slice(tile * TILE, (tile + 1) * TILE)
        key_rows = listed(table, fetched, tile, list_length, 0)
        value_rows = listed(table, fetched, tile, list_length, 1)
        scores = tile_scores(table, split_heads(queries[rows, :]), key_rows, tile, scale)
        probs = jnp.exp(scores - stats[:, tile : tile + 1])
        grad_probs = dot_nt(split_heads(grads[rows, :]), value_rows)
        grad_scores = (probs * (grad_probs - stats[:, tiles + tile : tiles + tile + 1])).astype(BF16)
        out[rows, :] = (join_heads(dot(grad_scores, key_rows)) * scale).astype(BF16)


def sum_kernel(chunk, arrived, mixed_part, grad_queries, out, total_of, sems):
    total = arrived[0, 0:chunk, :].astype(F32)
    for i in range(1, arrived.shape[0]):
        total += arrived[i, 0:chunk, :].astype(F32)
    total = total.astype(BF16)
    copies = total_of.shape[0]
    for i in range(copies):
        total_of[i] = total
    stores = []
    for at in range(out.shape[0] // copies):
        stores.append(pltpu.make_async_copy(total_of, out.at[pl.ds(at * copies, copies)], sems.at[at]))
        stores[-1].start()
    for store in stores:
        store.wait()


def owner_kernel(scale, chunk, group, table, fetched, arrived, keys, values, grad_keys, grad_values, key_sum, value_sum):
    tok_rows = keys.shape[0]
    senders = arrived.shape[0]
    key_tile = lax.broadcasted_iota(jnp.int32, (tok_rows, WIDTH), 0) // TILE
    key_sum[...] = jnp.zeros_like(key_sum)
    value_sum[...] = jnp.zeros_like(value_sum)

    def step(at, carry):
        query2, grad2, logs, deltas, keeps = [], [], [], [], []
        for k in range(group):
            i = at * group + k
            query2.append(split_heads(fetched[i, 2 * TILE : 3 * TILE, :]))
            grad2.append(split_heads(arrived[i, chunk : chunk + TILE, :]))
            parts = arrived[i, chunk + TILE : chunk + TILE + STAT_ROWS, :].astype(F32)
            logs.append(parts[0:1] + parts[1:2] + parts[2:3])
            deltas.append(parts[3:4] + parts[4:5] + parts[5:6])
            wanted = jnp.where(table[1, i] > 0, table[0, i], -1)
            keeps.append(key_tile == wanted)
        query2 = jnp.concatenate(query2, axis=0)
        grad2 = jnp.concatenate(grad2, axis=0)
        log_total = jnp.concatenate(logs, axis=1)
        delta = jnp.concatenate(deltas, axis=1)
        scores = dot_nt(keys[...], query2) * scale
        gaps = scores - log_total
        gaps = jnp.concatenate(
            [
                jnp.where(keeps[k], gaps[:, k * WIDTH : (k + 1) * WIDTH], -jnp.inf)
                for k in range(group)
            ],
            axis=1,
        )
        probs = jnp.exp(gaps)
        grad_probs = dot_nt(values[...], grad2)
        grad_scores = (probs * (grad_probs - delta)).astype(BF16)
        key_sum[...] += dot(grad_scores, query2)
        value_sum[...] += dot(probs.astype(BF16), grad2)
        return carry

    lax.fori_loop(0, senders // group, step, 0)
    grad_keys[...] = (key_sum[...] * scale).astype(BF16)
    grad_values[...] = value_sum[...].astype(BF16)


def assemble_kernel(gathered, out, staged, sems):
    tall = out.shape[0] // ROW_BLOCKS
    wide = out.shape[1] // COL_BLOCKS
    stores = []
    for at in range(COL_BLOCKS):
        for down in range(ROW_BLOCKS):
            for k in range(wide // WIDTH):
                column = at * wide + k * WIDTH
                staged[down * tall : (down + 1) * tall, column : column + WIDTH] = gathered[
                    at * ROW_BLOCKS + down, k * tall : (k + 1) * tall, :
                ]
        span = pl.ds(at * wide, wide)
        stores.append(pltpu.make_async_copy(staged.at[:, span], out.at[:, span], sems.at[at]))
        stores[-1].start()
    for store in stores:
        store.wait()


def exchange(blocks):
    return lax.all_to_all(blocks, "seq", split_axis=0, concat_axis=0, tiled=True)


def swap_cores(array):
    return lax.ppermute(array, "core", [(0, 1), (1, 0)])


def swap_chips(array, apart):
    return lax.ppermute(array, "z", [(z, z ^ apart) for z in range(lax.axis_size("z"))])


def body(queries, keys, values, out_weight, grad_mixed, kv_tiles, kv_counts):
    tok_rows, row_width = queries.shape
    tiles_dev = tok_rows // TILE
    list_length = kv_tiles.shape[1]
    seq_count = lax.axis_size("seq")
    scale = 1.0 / math.sqrt(HD)
    model = out_weight.shape[1]
    chunk = model // seq_count
    device = lax.axis_index("seq")
    block = jax.ShapeDtypeStruct((tok_rows, row_width), BF16)

    grad_t = lax.all_gather(grad_mixed.T, "z", axis=0, tiled=True)
    lists = kv_tiles.T
    groups = 4
    outgoing, table = pl.pallas_call(
        pack_kernel,
        out_shape=(
            pltpu.HBM((seq_count, 3 * TILE, row_width), BF16),
            jax.ShapeDtypeStruct((5, seq_count), jnp.int32),
        ),
        in_specs=[SMEM, HBM, HBM, HBM, HBM, HBM],
        out_specs=(HBM, SMEM),
        scratch_shapes=[
            pltpu.SMEM(lists.shape, jnp.int32),
            pltpu.SMEM((1,) + kv_counts.shape, jnp.int32),
            pltpu.VMEM(lists.shape, jnp.int32),
            pltpu.VMEM((1,) + kv_counts.shape, jnp.int32),
            pltpu.VMEM((groups, seq_count // groups, 3 * TILE, row_width), BF16),
            pltpu.VMEM(lists.shape, jnp.int32),
            pltpu.SMEM(lists.shape, jnp.int32),
            pltpu.VMEM((3, tok_rows, row_width), BF16),
            pltpu.SemaphoreType.DMA((8 + groups,)),
        ],
        compiler_params=PARAMS,
        name="pack",
    )(
        device[None].astype(jnp.int32),
        stay(lists),
        stay(kv_counts[None, :]),
        stay(queries),
        stay(keys),
        stay(values),
    )
    fetched = exchange(outgoing)
    other_t = swap_cores(grad_t)
    core = lax.axis_index("core")[None].astype(jnp.int32)

    second, attention, grads, stats = pl.pallas_call(
        functools.partial(forward_kernel, scale, list_length),
        out_shape=(
            pltpu.HBM((seq_count, chunk + TILE + STAT_ROWS, row_width), BF16),
            block,
            block,
            jax.ShapeDtypeStruct((WIDTH, WIDTH), F32),
        ),
        in_specs=[SMEM, VMEM, VMEM, SMEM, HBM, HBM, HBM],
        out_specs=(HBM, VMEM, VMEM, VMEM),
        scratch_shapes=[
            pltpu.VMEM((model, tok_rows), BF16),
            pltpu.VMEM(out_weight.shape, BF16),
            pltpu.VMEM((tiles_dev, TILE + STAT_ROWS, row_width), BF16),
            pltpu.VMEM((seq_count, chunk + TILE + STAT_ROWS, row_width), BF16),
            pltpu.SemaphoreType.DMA((COL_BLOCKS + GATHERED,)),
        ],
        compiler_params=PARAMS,
        name="forward",
    )(table, fetched, queries, core, stay(grad_t), stay(other_t), stay(out_weight))
    arrived = exchange(second)

    run = grad_mixed.shape[1]
    blocks = model // run // 2
    shares = jax.ShapeDtypeStruct((blocks, run, tok_rows), BF16)
    mine, sent = pl.pallas_call(
        mixed_kernel,
        out_shape=(shares, shares),
        in_specs=[SMEM, HBM, VMEM],
        out_specs=(VMEM, VMEM),
        scratch_shapes=[pltpu.VMEM(out_weight.shape, BF16), pltpu.SemaphoreType.DMA],
        compiler_params=PARAMS,
        name="mixed_share",
    )(core, stay(out_weight), attention)
    far = blocks // NEAR
    mine, *sent = pl.pallas_call(
        pair_kernel,
        out_shape=(jax.ShapeDtypeStruct((far, run, tok_rows), F32),)
        + (jax.ShapeDtypeStruct((far, run, tok_rows), BF16),) * (NEAR - 1),
        in_specs=[SMEM, VMEM, VMEM],
        out_specs=(VMEM,) * NEAR,
        compiler_params=PARAMS,
        name="mixed_pair",
    )(lax.axis_index("z")[None].astype(jnp.int32), mine, swap_cores(sent))
    mine, sent = pl.pallas_call(
        near_kernel,
        out_shape=(
            jax.ShapeDtypeStruct((run, tok_rows), F32),
            jax.ShapeDtypeStruct((run, tok_rows), BF16),
        ),
        in_specs=[VMEM] * NEAR,
        out_specs=(VMEM, VMEM),
        compiler_params=PARAMS,
        name="mixed_near",
    )(mine, *(swap_chips(part, near + 1) for near, part in enumerate(sent)))

    grad_queries = pl.pallas_call(
        functools.partial(query_kernel, scale, list_length),
        out_shape=block,
        in_specs=[SMEM, VMEM, VMEM, VMEM, VMEM],
        out_specs=VMEM,
        compiler_params=PARAMS,
        cost_estimate=pl.CostEstimate(flops=400_000_000, bytes_accessed=4_000_000, transcendentals=300_000),
        name="query_grad",
    )(table, fetched, queries, grads, stats)

    third = pl.pallas_call(
        functools.partial(sum_kernel, chunk),
        out_shape=pltpu.HBM((seq_count, chunk, row_width), BF16),
        in_specs=[VMEM, ANY, ANY],
        out_specs=HBM,
        scratch_shapes=[pltpu.VMEM((4, chunk, row_width), BF16), pltpu.SemaphoreType.DMA((seq_count // 4,))],
        compiler_params=PARAMS,
        name="sum_share",
    )(arrived, sent, grad_queries)
    gathered = exchange(third)

    grad_keys, grad_values = pl.pallas_call(
        functools.partial(owner_kernel, scale, chunk, 4),
        out_shape=(block, block),
        in_specs=[SMEM, VMEM, VMEM, VMEM, VMEM],
        out_specs=(VMEM, VMEM),
        scratch_shapes=[pltpu.VMEM((tok_rows, row_width), F32), pltpu.VMEM((tok_rows, row_width), F32)],
        compiler_params=PARAMS,
        cost_estimate=pl.CostEstimate(flops=1_100_000_000, bytes_accessed=4_000_000, transcendentals=1_000_000),
        name="owner_grad",
    )(table, fetched, arrived, keys, values)
    mixed = pl.pallas_call(
        last_kernel,
        out_shape=jax.ShapeDtypeStruct((run, tok_rows), BF16),
        in_specs=[VMEM, VMEM, ANY],
        out_specs=VMEM,
        compiler_params=PARAMS,
        name="mixed_last",
    )(mine, swap_chips(sent, 4), grad_keys).T
    weight_grad = pl.pallas_call(
        assemble_kernel,
        out_shape=pltpu.HBM(out_weight.shape, BF16),
        in_specs=[VMEM],
        out_specs=HBM,
        scratch_shapes=[
            pltpu.VMEM(out_weight.shape, BF16),
            pltpu.SemaphoreType.DMA((COL_BLOCKS,)),
        ],
        compiler_params=PARAMS,
        name="assemble",
    )(gathered)
    return (mixed, grad_queries, grad_keys, grad_values, weight_grad)


def solution(mesh):
    seq_count, head_count = mesh.devices.shape
    split = Mesh(mesh.devices.reshape(seq_count, head_count // 2, 2), ("seq", "z", "core"))
    both = P("seq", ("z", "core"))
    rows = P(("z", "core"), None)
    return jax.shard_map(
        body,
        mesh=split,
        in_specs=(both, both, both, rows, both, P(), P()),
        out_specs=(both, both, both, both, rows),
        check_vma=False,
    )
```

```python
import functools
import math

import jax
import jax.numpy as jnp
from jax import lax
from jax.experimental import pallas as pl
from jax.experimental.pallas import tpu as pltpu
from jax.sharding import Mesh, PartitionSpec as P

TILE = 64
HD = 64
WIDTH = 2 * HD
STAT_ROWS = 8
FEW = 8
GATHERED = 16
BF16 = jnp.bfloat16
F32 = jnp.float32
VMEM = pl.BlockSpec(memory_space=pltpu.VMEM)
SMEM = pl.BlockSpec(memory_space=pltpu.SMEM)
HBM = pl.BlockSpec(memory_space=pltpu.HBM)
ANY = pl.BlockSpec(memory_space=pl.ANY)
PARAMS = pltpu.CompilerParams(vmem_limit_bytes=16 * 1024 * 1024)
NT = (((1,), (1,)), ((), ()))


def stay(array):
    return pltpu.with_memory_space_constraint(array, pltpu.HBM)


def dot(a, b):
    return jnp.dot(a, b, preferred_element_type=F32)


def dot_nt(a, b):
    return lax.dot_general(a, b, NT, preferred_element_type=F32)


def split_heads(rows):
    lane = lax.broadcasted_iota(jnp.int32, rows.shape, 1)
    zero = jnp.zeros_like(rows)
    return jnp.concatenate(
        [jnp.where(lane < HD, rows, zero), jnp.where(lane < HD, zero, rows)], axis=0
    )


def join_heads(rows):
    half = rows.shape[0] // 2
    lane = lax.broadcasted_iota(jnp.int32, (half, rows.shape[1]), 1)
    return jnp.where(lane < HD, rows[:half], rows[half:])


def pack_kernel(
    place, lists_h, counts_h, queries, keys, values, out, table,
    lists, counts, lists_v, counts_v, staged, codes_v, codes, held, sems,
):
    list_length, tile_count = lists_v.shape
    seq_count = out.shape[0]
    tiles = tile_count // seq_count
    device = place[0]
    pairs = (
        (lists_h, lists_v), (counts_h, counts_v), (lists_h, lists), (counts_h, counts),
        (keys, held.at[0]), (values, held.at[1]), (queries, held.at[2]),
    )
    loads = [pltpu.make_async_copy(*pair, sems.at[k]) for k, pair in enumerate(pairs)]
    for load in loads:
        load.start()
    for load in loads[:2]:
        load.wait()
    listed_tile = lists_v[...]
    entry = lax.broadcasted_iota(jnp.int32, listed_tile.shape, 0)
    code = lax.rem(listed_tile, tiles) + jnp.where(entry < counts_v[...], tiles, 0)
    code = jnp.where(lax.div(listed_tile, tiles) == device, code, 0)
    code = jnp.broadcast_to(jnp.sum(code, axis=0, keepdims=True), code.shape)
    codes_v[...] = sum(
        (pltpu.roll(code, tile_count - tile, 1) for tile in range(1, tiles)), start=code
    )
    scalars = pltpu.make_async_copy(codes_v, codes, sems.at[7])
    scalars.start()
    for load in loads[2:4]:
        load.wait()
    for tile in range(tiles):
        table[4, tile] = counts[0, device * tiles + tile]
        for j in range(list_length):
            owner = lax.div(lists[j, device * tiles + tile], tiles)
            table[2, tile * list_length + j] = owner
            table[3, owner] = tile
    groups = staged.shape[0]
    loads[6].wait()
    for i in range(seq_count):
        mine = pl.ds(pl.multiple_of(table[3, i] * TILE, TILE), TILE)
        staged[i * groups // seq_count, i % (seq_count // groups), 2 * TILE : 3 * TILE, :] = held[2, mine, :]
    scalars.wait()
    for load in loads[4:6]:
        load.wait()
    stores = []
    for group in range(groups):
        for k in range(seq_count // groups):
            i = group * (seq_count // groups) + k
            code = codes[0, i * tiles]
            asked = lax.rem(code, tiles)
            table[0, i] = asked
            table[1, i] = lax.div(code, tiles)
            tile = pl.ds(pl.multiple_of(asked * TILE, TILE), TILE)
            staged[group, k, 0:TILE, :] = held[0, tile, :]
            staged[group, k, TILE : 2 * TILE, :] = held[1, tile, :]
        span = pl.ds(group * (seq_count // groups), seq_count // groups)
        stores.append(pltpu.make_async_copy(staged.at[group], out.at[span], sems.at[8 + group]))
        stores[-1].start()
    for store in stores:
        store.wait()


def joined(core, own, other, z):
    run = 2 * own.shape[0] // GATHERED
    mine, theirs = own[z * run : (z + 1) * run, :], other[z * run : (z + 1) * run, :]
    first = core == 0
    return jnp.concatenate([jnp.where(first, mine, theirs), jnp.where(first, theirs, mine)], axis=0)


def grad_kernel(core, own, other, weight_h, grads, weight, sem):
    load = pltpu.make_async_copy(weight_h, weight, sem)
    load.start()
    load.wait()
    wide = 2 * weight.shape[1] // GATHERED
    total = jnp.zeros((WIDTH, grads.shape[0]), F32)
    for z in range(GATHERED // 2):
        total += dot(weight[:, z * wide : (z + 1) * wide], joined(core[0], own, other, z))
    grads[...] = total.T.astype(BF16)


def mixed_kernel(core, weight_h, attention, keep, send, weight, sem):
    load = pltpu.make_async_copy(weight_h, weight, sem)
    load.start()
    load.wait()
    chips, run = keep.shape[0], keep.shape[1]
    weight_t = weight[...].T
    first_core = core[0] == 0
    for z in range(chips):
        shares = [
            dot_nt(weight_t[(2 * z + k) * run : (2 * z + k + 1) * run], attention[...]).astype(BF16)
            for k in range(2)
        ]
        keep[z] = jnp.where(first_core, shares[0], shares[1])
        send[z] = jnp.where(first_core, shares[1], shares[0])


def pair_kernel(place, mine, arrived, keep, next_1, back_1, next_2, back_2):
    chips = mine.shape[0]
    homes = {
        0: (keep, 0), 4: (keep, 1), 1: (next_1, 0), 5: (next_1, 1),
        7: (back_1, 0), 3: (back_1, 1), 2: (next_2, 0), 6: (back_2, 0),
    }
    for z in range(chips):
        total = mine[z].astype(F32) + arrived[z].astype(F32)
        apart = lax.rem(z + chips - place[0], chips)
        for distance, (target, slot) in homes.items():

            @pl.when(apart == distance)
            def _(target=target, slot=slot):
                target[slot] = total.astype(target.dtype)


def near_kernel(mine, next_1, back_1, next_2, back_2, keep, send):
    here, opposite = (mine[i] + next_1[i].astype(F32) + back_1[i].astype(F32) for i in range(2))
    keep[...] = here + next_2[0].astype(F32) + back_2[0].astype(F32)
    send[...] = opposite.astype(BF16)


def last_kernel(mine, arrived, grad_keys, out):
    out[...] = (mine[...] + arrived[...].astype(F32)).astype(BF16)


def listed(table, fetched, tile, list_length, part):
    return jnp.concatenate(
        [
            fetched[table[2, tile * list_length + j], part * TILE : (part + 1) * TILE, :]
            for j in range(list_length)
        ],
        axis=0,
    )


def tile_scores(table, query2, key_rows, tile, scale):
    scores = dot_nt(query2, key_rows) * scale
    column = lax.broadcasted_iota(jnp.int32, scores.shape, 1)
    return jnp.where(column < table[4, tile] * TILE, scores, -jnp.inf)


def forward_kernel(
    scale, list_length, table, fetched, queries, core, own, other, grads, out, attention, stats,
    spread, staged, sems,
):
    tiles = queries.shape[0] // TILE
    seq_count = out.shape[0]
    model = 2 * own.shape[0]
    chunk = model // seq_count
    lane = lax.broadcasted_iota(jnp.int32, (WIDTH, WIDTH), 1)
    table_of_stats = jnp.zeros((WIDTH, WIDTH), F32)
    for tile in range(tiles):
        rows = slice(tile * TILE, (tile + 1) * TILE)
        query2 = split_heads(queries[rows, :])
        key_rows = listed(table, fetched, tile, list_length, 0)
        value_rows = listed(table, fetched, tile, list_length, 1)
        scores = tile_scores(table, query2, key_rows, tile, scale)
        top = jnp.max(scores, axis=1, keepdims=True)
        log_total = top + jnp.log(jnp.sum(jnp.exp(scores - top), axis=1, keepdims=True))
        weights = jnp.exp(scores - log_total).astype(BF16)
        attended = join_heads(dot(weights, value_rows)).astype(BF16)
        attention[rows, :] = attended
        product = grads[rows, :].astype(F32) * attended.astype(F32)
        delta = jnp.sum(split_heads(product), axis=1, keepdims=True)
        table_of_stats = jnp.where(lane == tile, log_total, table_of_stats)
        table_of_stats = jnp.where(lane == tiles + tile, delta, table_of_stats)
    stats[...] = table_of_stats
    by_row = table_of_stats.T
    row = lax.broadcasted_iota(jnp.int32, (STAT_ROWS, WIDTH), 0)
    for tile in range(tiles):
        block = jnp.zeros((STAT_ROWS, WIDTH), F32)
        for at, value in ((0, by_row[tile : tile + 1]), (3, by_row[tiles + tile : tiles + tile + 1])):
            for part in range(3):
                rounded = value.astype(BF16).astype(F32)
                block = jnp.where(row == at + part, rounded, block)
                value = value - rounded
        spread[tile, 0:TILE, :] = grads[tile * TILE : (tile + 1) * TILE, :]
        spread[tile, TILE : TILE + STAT_ROWS, :] = block.astype(BF16)

    for i in range(seq_count):
        staged[i, chunk : chunk + TILE + STAT_ROWS, :] = spread[table[3, i]]
    attention_t = attention[...].astype(F32).T.astype(BF16)
    across = seq_count * FEW // WIDTH
    steps = GATHERED // 4
    stores = []
    for at in range(steps):
        rows = jnp.concatenate([joined(core[0], own, other, 2 * at + k) for k in range(2)], axis=0)
        part = dot_nt(attention_t, rows)
        run = at * across // steps
        first = (at - run * steps // across) * rows.shape[0] // WIDTH * FEW
        for down in range(WIDTH // FEW):
            lines = part[down * FEW : (down + 1) * FEW, :]
            for k in range(0, rows.shape[0], 2 * WIDTH):
                pair = jnp.concatenate([lines[:, k : k + WIDTH], lines[:, k + WIDTH : k + 2 * WIDTH]], axis=0)
                start = first + k // WIDTH * FEW
                staged[down * across + run, start : start + 2 * FEW, :] = pair.astype(BF16)
        if (at + 1) * across % steps == 0:
            for down in range(WIDTH // FEW):
                c = down * across + run
                stores.append(pltpu.make_async_copy(staged.at[c], out.at[c], sems.at[c]))
                stores[-1].start()
    for store in stores:
        store.wait()


def query_kernel(scale, list_length, table, fetched, queries, grads, stats, out):
    tiles = queries.shape[0] // TILE
    for tile in range(tiles):
        rows = slice(tile * TILE, (tile + 1) * TILE)
        key_rows = listed(table, fetched, tile, list_length, 0)
        value_rows = listed(table, fetched, tile, list_length, 1)
        scores = tile_scores(table, split_heads(queries[rows, :]), key_rows, tile, scale)
        probs = jnp.exp(scores - stats[:, tile : tile + 1])
        grad_probs = dot_nt(split_heads(grads[rows, :]), value_rows)
        grad_scores = (probs * (grad_probs - stats[:, tiles + tile : tiles + tile + 1])).astype(BF16)
        out[rows, :] = (join_heads(dot(grad_scores, key_rows)) * scale).astype(BF16)


def sum_kernel(chunk, arrived, mixed_part, grad_queries, out, total_of, sems):
    total = arrived[0, 0:chunk, :].astype(F32)
    for i in range(1, arrived.shape[0]):
        total += arrived[i, 0:chunk, :].astype(F32)
    total = total.astype(BF16)
    copies = total_of.shape[0]
    for i in range(copies):
        total_of[i] = total
    stores = []
    for at in range(out.shape[0] // copies):
        stores.append(pltpu.make_async_copy(total_of, out.at[pl.ds(at * copies, copies)], sems.at[at]))
        stores[-1].start()
    for store in stores:
        store.wait()


def owner_kernel(scale, chunk, group, table, fetched, arrived, keys, values, grad_keys, grad_values, key_sum, value_sum):
    tok_rows = keys.shape[0]
    senders = arrived.shape[0]
    key_tile = lax.broadcasted_iota(jnp.int32, (tok_rows, WIDTH), 0) // TILE
    key_sum[...] = jnp.zeros_like(key_sum)
    value_sum[...] = jnp.zeros_like(value_sum)

    def step(at, carry):
        query2, grad2, logs, deltas, keeps = [], [], [], [], []
        for k in range(group):
            i = at * group + k
            query2.append(split_heads(fetched[i, 2 * TILE : 3 * TILE, :]))
            grad2.append(split_heads(arrived[i, chunk : chunk + TILE, :]))
            parts = arrived[i, chunk + TILE : chunk + TILE + STAT_ROWS, :].astype(F32)
            logs.append(parts[0:1] + parts[1:2] + parts[2:3])
            deltas.append(parts[3:4] + parts[4:5] + parts[5:6])
            wanted = jnp.where(table[1, i] > 0, table[0, i], -1)
            keeps.append(key_tile == wanted)
        query2 = jnp.concatenate(query2, axis=0)
        grad2 = jnp.concatenate(grad2, axis=0)
        log_total = jnp.concatenate(logs, axis=1)
        delta = jnp.concatenate(deltas, axis=1)
        scores = dot_nt(keys[...], query2) * scale
        gaps = scores - log_total
        gaps = jnp.concatenate(
            [
                jnp.where(keeps[k], gaps[:, k * WIDTH : (k + 1) * WIDTH], -jnp.inf)
                for k in range(group)
            ],
            axis=1,
        )
        probs = jnp.exp(gaps)
        grad_probs = dot_nt(values[...], grad2)
        grad_scores = (probs * (grad_probs - delta)).astype(BF16)
        key_sum[...] += dot(grad_scores, query2)
        value_sum[...] += dot(probs.astype(BF16), grad2)
        return carry

    lax.fori_loop(0, senders // group, step, 0)
    grad_keys[...] = (key_sum[...] * scale).astype(BF16)
    grad_values[...] = value_sum[...].astype(BF16)


def exchange(blocks):
    return lax.all_to_all(blocks, "seq", split_axis=0, concat_axis=0, tiled=True)


def swap_cores(array):
    return lax.ppermute(array, "core", [(0, 1), (1, 0)])


def to_chip(array, apart):
    chips = lax.axis_size("z")
    return lax.ppermute(array, "z", [(z, (z + apart) % chips) for z in range(chips)])


def body(queries, keys, values, out_weight, grad_mixed, kv_tiles, kv_counts):
    tok_rows, row_width = queries.shape
    tiles_dev = tok_rows // TILE
    list_length = kv_tiles.shape[1]
    seq_count = lax.axis_size("seq")
    scale = 1.0 / math.sqrt(HD)
    model = out_weight.shape[1]
    chunk = model // seq_count
    device = lax.axis_index("seq")
    block = jax.ShapeDtypeStruct((tok_rows, row_width), BF16)

    grad_t = lax.all_gather(grad_mixed.T, "z", axis=0, tiled=True)
    lists = kv_tiles.T
    groups = 4
    outgoing, table = pl.pallas_call(
        pack_kernel,
        out_shape=(
            pltpu.HBM((seq_count, 3 * TILE, row_width), BF16),
            jax.ShapeDtypeStruct((5, seq_count), jnp.int32),
        ),
        in_specs=[SMEM, HBM, HBM, HBM, HBM, HBM],
        out_specs=(HBM, SMEM),
        scratch_shapes=[
            pltpu.SMEM(lists.shape, jnp.int32),
            pltpu.SMEM((1,) + kv_counts.shape, jnp.int32),
            pltpu.VMEM(lists.shape, jnp.int32),
            pltpu.VMEM((1,) + kv_counts.shape, jnp.int32),
            pltpu.VMEM((groups, seq_count // groups, 3 * TILE, row_width), BF16),
            pltpu.VMEM(lists.shape, jnp.int32),
            pltpu.SMEM(lists.shape, jnp.int32),
            pltpu.VMEM((3, tok_rows, row_width), BF16),
            pltpu.SemaphoreType.DMA((8 + groups,)),
        ],
        compiler_params=PARAMS,
        name="pack",
    )(
        device[None].astype(jnp.int32),
        stay(lists),
        stay(kv_counts[None, :]),
        stay(queries),
        stay(keys),
        stay(values),
    )
    fetched = exchange(outgoing)
    other_t = swap_cores(grad_t)
    core = lax.axis_index("core")[None].astype(jnp.int32)

    grads = pl.pallas_call(
        grad_kernel,
        out_shape=block,
        in_specs=[SMEM, VMEM, VMEM, HBM],
        out_specs=VMEM,
        scratch_shapes=[pltpu.VMEM(out_weight.shape, BF16), pltpu.SemaphoreType.DMA],
        compiler_params=PARAMS,
        cost_estimate=pl.CostEstimate(flops=3_000_000_000, bytes_accessed=3_000_000, transcendentals=0),
        name="attention_grad",
    )(core, grad_t, other_t, stay(out_weight))

    second, attention, stats = pl.pallas_call(
        functools.partial(forward_kernel, scale, list_length),
        out_shape=(
            pltpu.HBM((seq_count, chunk + TILE + STAT_ROWS, row_width), BF16),
            block,
            jax.ShapeDtypeStruct((WIDTH, WIDTH), F32),
        ),
        in_specs=[SMEM, VMEM, VMEM, SMEM, VMEM, VMEM, VMEM],
        out_specs=(HBM, VMEM, VMEM),
        scratch_shapes=[
            pltpu.VMEM((tiles_dev, TILE + STAT_ROWS, row_width), BF16),
            pltpu.VMEM((seq_count, chunk + TILE + STAT_ROWS, row_width), BF16),
            pltpu.SemaphoreType.DMA((seq_count,)),
        ],
        compiler_params=PARAMS,
        name="forward",
    )(table, fetched, queries, core, grad_t, other_t, grads)
    arrived = exchange(second)

    run = grad_mixed.shape[1]
    blocks = model // run // 2
    shares = jax.ShapeDtypeStruct((blocks, run, tok_rows), BF16)
    mine, sent = pl.pallas_call(
        mixed_kernel,
        out_shape=(shares, shares),
        in_specs=[SMEM, HBM, VMEM],
        out_specs=(VMEM, VMEM),
        scratch_shapes=[pltpu.VMEM(out_weight.shape, BF16), pltpu.SemaphoreType.DMA],
        compiler_params=PARAMS,
        name="mixed_share",
    )(core, stay(out_weight), attention)
    mine, *sent = pl.pallas_call(
        pair_kernel,
        out_shape=(
            jax.ShapeDtypeStruct((2, run, tok_rows), F32),
            jax.ShapeDtypeStruct((2, run, tok_rows), BF16),
            jax.ShapeDtypeStruct((2, run, tok_rows), BF16),
            jax.ShapeDtypeStruct((1, run, tok_rows), BF16),
            jax.ShapeDtypeStruct((1, run, tok_rows), BF16),
        ),
        in_specs=[SMEM, VMEM, VMEM],
        out_specs=(VMEM,) * 5,
        compiler_params=PARAMS,
        name="mixed_pair",
    )(lax.axis_index("z")[None].astype(jnp.int32), mine, swap_cores(sent))
    mine, sent = pl.pallas_call(
        near_kernel,
        out_shape=(
            jax.ShapeDtypeStruct((run, tok_rows), F32),
            jax.ShapeDtypeStruct((run, tok_rows), BF16),
        ),
        in_specs=[VMEM] * 5,
        out_specs=(VMEM, VMEM),
        compiler_params=PARAMS,
        name="mixed_near",
    )(mine, *(to_chip(part, apart) for part, apart in zip(sent, (1, -1, 2, -2), strict=True)))

    grad_queries = pl.pallas_call(
        functools.partial(query_kernel, scale, list_length),
        out_shape=block,
        in_specs=[SMEM, VMEM, VMEM, VMEM, VMEM],
        out_specs=VMEM,
        compiler_params=PARAMS,
        cost_estimate=pl.CostEstimate(flops=400_000_000, bytes_accessed=4_000_000, transcendentals=300_000),
        name="query_grad",
    )(table, fetched, queries, grads, stats)

    third = pl.pallas_call(
        functools.partial(sum_kernel, chunk),
        out_shape=pltpu.HBM((seq_count, chunk, row_width), BF16),
        in_specs=[VMEM, ANY, HBM],
        out_specs=HBM,
        scratch_shapes=[pltpu.VMEM((4, chunk, row_width), BF16), pltpu.SemaphoreType.DMA((seq_count // 4,))],
        compiler_params=PARAMS,
        name="sum_share",
    )(arrived, sent, stay(grad_queries))
    gathered = exchange(third)

    grad_keys, grad_values = pl.pallas_call(
        functools.partial(owner_kernel, scale, chunk, 4),
        out_shape=(block, block),
        in_specs=[SMEM, VMEM, VMEM, VMEM, VMEM],
        out_specs=(VMEM, VMEM),
        scratch_shapes=[pltpu.VMEM((tok_rows, row_width), F32), pltpu.VMEM((tok_rows, row_width), F32)],
        compiler_params=PARAMS,
        cost_estimate=pl.CostEstimate(flops=1_100_000_000, bytes_accessed=4_000_000, transcendentals=1_000_000),
        name="owner_grad",
    )(table, fetched, arrived, keys, values)
    mixed = pl.pallas_call(
        last_kernel,
        out_shape=jax.ShapeDtypeStruct((run, tok_rows), BF16),
        in_specs=[VMEM, VMEM, HBM],
        out_specs=VMEM,
        compiler_params=PARAMS,
        name="mixed_last",
    )(mine, to_chip(sent, 4), stay(grad_keys)).T
    weight_grad = (
        gathered.reshape(row_width // FEW, seq_count * FEW // row_width, chunk // FEW, FEW, WIDTH)
        .transpose(0, 3, 1, 2, 4)
        .reshape(out_weight.shape)
    )
    return (mixed, grad_queries, grad_keys, grad_values, weight_grad)


def solution(mesh):
    seq_count, head_count = mesh.devices.shape
    split = Mesh(mesh.devices.reshape(seq_count, head_count // 2, 2), ("seq", "z", "core"))
    both = P("seq", ("z", "core"))
    rows = P(("z", "core"), None)
    return jax.shard_map(
        body,
        mesh=split,
        in_specs=(both, both, both, rows, both, P(), P()),
        out_specs=(both, both, both, both, rows),
        check_vma=False,
    )
```

```python
import functools
import math

import jax
import jax.numpy as jnp
from jax import lax
from jax.experimental import pallas as pl
from jax.experimental.pallas import tpu as pltpu
from jax.sharding import Mesh, PartitionSpec as P

TILE = 64
HD = 64
WIDTH = 2 * HD
STAT_ROWS = 8
FEW = 8
GATHERED = 16
BF16 = jnp.bfloat16
F32 = jnp.float32
VMEM = pl.BlockSpec(memory_space=pltpu.VMEM)
SMEM = pl.BlockSpec(memory_space=pltpu.SMEM)
HBM = pl.BlockSpec(memory_space=pltpu.HBM)
ANY = pl.BlockSpec(memory_space=pl.ANY)
PARAMS = pltpu.CompilerParams(vmem_limit_bytes=16 * 1024 * 1024)
NT = (((1,), (1,)), ((), ()))


def stay(array):
    return pltpu.with_memory_space_constraint(array, pltpu.HBM)


def dot(a, b):
    return jnp.dot(a, b, preferred_element_type=F32)


def dot_nt(a, b):
    return lax.dot_general(a, b, NT, preferred_element_type=F32)


def split_heads(rows):
    lane = lax.broadcasted_iota(jnp.int32, rows.shape, 1)
    zero = jnp.zeros_like(rows)
    return jnp.concatenate(
        [jnp.where(lane < HD, rows, zero), jnp.where(lane < HD, zero, rows)], axis=0
    )


def join_heads(rows):
    half = rows.shape[0] // 2
    lane = lax.broadcasted_iota(jnp.int32, (half, rows.shape[1]), 1)
    return jnp.where(lane < HD, rows[:half], rows[half:])


def pack_kernel(
    place, lists_h, counts_h, queries, keys, values, out, table,
    lists, counts, lists_v, counts_v, staged, asking, codes_v, codes, held, sems,
):
    list_length, tile_count = lists_v.shape
    seq_count = out.shape[0]
    tiles = tile_count // seq_count
    device = place[0]
    pairs = (
        (lists_h, lists_v), (counts_h, counts_v), (lists_h, lists), (counts_h, counts),
        (keys, held.at[0]), (values, held.at[1]), (queries, held.at[2]),
    )
    loads = [pltpu.make_async_copy(*pair, sems.at[k]) for k, pair in enumerate(pairs)]
    for load in loads:
        load.start()
    for load in loads[:2]:
        load.wait()
    listed_tile = lists_v[...]
    entry = lax.broadcasted_iota(jnp.int32, listed_tile.shape, 0)
    code = lax.rem(listed_tile, tiles) + jnp.where(entry < counts_v[...], tiles, 0)
    code = jnp.where(lax.div(listed_tile, tiles) == device, code, 0)
    code = jnp.broadcast_to(jnp.sum(code, axis=0, keepdims=True), code.shape)
    codes_v[...] = sum(
        (pltpu.roll(code, tile_count - tile, 1) for tile in range(1, tiles)), start=code
    )
    scalars = pltpu.make_async_copy(codes_v, codes, sems.at[7])
    scalars.start()
    for load in loads[2:4]:
        load.wait()
    for tile in range(tiles):
        table[4, tile] = counts[0, device * tiles + tile]
        for j in range(list_length):
            owner = lax.div(lists[j, device * tiles + tile], tiles)
            table[2, tile * list_length + j] = owner
            table[3, owner] = tile
    groups = sems.shape[0] - 9
    each = seq_count // groups
    loads[6].wait()
    for i in range(seq_count):
        mine = pl.ds(pl.multiple_of(table[3, i] * TILE, TILE), TILE)
        asking[i] = held[2, mine, :]
    stores = [pltpu.make_async_copy(asking, out.at[:, pl.ds(2 * TILE, TILE), :], sems.at[8])]
    stores[0].start()
    scalars.wait()
    for load in loads[4:6]:
        load.wait()
    for group in range(groups):
        span = pl.ds(group * each, each)
        for i in range(group * each, (group + 1) * each):
            code = codes[0, i * tiles]
            asked = lax.rem(code, tiles)
            table[0, i] = asked
            table[1, i] = lax.div(code, tiles)
            tile = pl.ds(pl.multiple_of(asked * TILE, TILE), TILE)
            staged[i, 0:TILE, :] = held[0, tile, :]
            staged[i, TILE : 2 * TILE, :] = held[1, tile, :]
        stores.append(
            pltpu.make_async_copy(staged.at[span], out.at[span, pl.ds(0, 2 * TILE), :], sems.at[9 + group])
        )
        stores[-1].start()
    for store in stores:
        store.wait()


def joined(core, own, other, z):
    run = 2 * own.shape[0] // GATHERED
    mine, theirs = own[z * run : (z + 1) * run, :], other[z * run : (z + 1) * run, :]
    first = core == 0
    return jnp.concatenate([jnp.where(first, mine, theirs), jnp.where(first, theirs, mine)], axis=0)


def grad_kernel(core, own, other, weight_h, grads, weight, sem):
    load = pltpu.make_async_copy(weight_h, weight, sem)
    load.start()
    load.wait()
    wide = 2 * weight.shape[1] // GATHERED
    total = jnp.zeros((WIDTH, grads.shape[0]), F32)
    for z in range(GATHERED // 2):
        total += dot(weight[:, z * wide : (z + 1) * wide], joined(core[0], own, other, z))
    grads[...] = total.T.astype(BF16)


def mixed_kernel(core, weight_h, attention, keep, send, weight, sem):
    load = pltpu.make_async_copy(weight_h, weight, sem)
    load.start()
    load.wait()
    chips, run = keep.shape[0], keep.shape[1]
    weight_t = weight[...].T
    first_core = core[0] == 0
    for z in range(chips):
        shares = [
            dot_nt(weight_t[(2 * z + k) * run : (2 * z + k + 1) * run], attention[...]).astype(BF16)
            for k in range(2)
        ]
        keep[z] = jnp.where(first_core, shares[0], shares[1])
        send[z] = jnp.where(first_core, shares[1], shares[0])


def pair_kernel(place, mine, arrived, keep, next_1, back_1, next_2, back_2):
    chips = mine.shape[0]
    homes = {
        0: (keep, 0), 4: (keep, 1), 1: (next_1, 0), 5: (next_1, 1),
        7: (back_1, 0), 3: (back_1, 1), 2: (next_2, 0), 6: (back_2, 0),
    }
    for z in range(chips):
        total = mine[z].astype(F32) + arrived[z].astype(F32)
        apart = lax.rem(z + chips - place[0], chips)
        for distance, (target, slot) in homes.items():

            @pl.when(apart == distance)
            def _(target=target, slot=slot):
                target[slot] = total.astype(target.dtype)


def near_kernel(mine, next_1, back_1, next_2, back_2, keep, send):
    here, opposite = (mine[i] + next_1[i].astype(F32) + back_1[i].astype(F32) for i in range(2))
    keep[...] = here + next_2[0].astype(F32) + back_2[0].astype(F32)
    send[...] = opposite.astype(BF16)


def last_kernel(mine, arrived, grad_keys, out):
    out[...] = (mine[...] + arrived[...].astype(F32)).astype(BF16)


def listed(table, fetched, tile, list_length, part):
    return jnp.concatenate(
        [
            fetched[table[2, tile * list_length + j], part * TILE : (part + 1) * TILE, :]
            for j in range(list_length)
        ],
        axis=0,
    )


def tile_scores(table, query2, key_rows, tile, scale):
    scores = dot_nt(query2, key_rows) * scale
    column = lax.broadcasted_iota(jnp.int32, scores.shape, 1)
    return jnp.where(column < table[4, tile] * TILE, scores, -jnp.inf)


def forward_kernel(
    scale, list_length, table, fetched, queries, core, own, other, grads, out, attention, stats, requests,
    spread, staged, sems,
):
    tiles = queries.shape[0] // TILE
    seq_count = out.shape[0]
    asked = pltpu.make_async_copy(fetched.at[:, pl.ds(2 * TILE, TILE), :], requests, sems.at[seq_count])
    asked.start()
    model = 2 * own.shape[0]
    chunk = model // seq_count
    lane = lax.broadcasted_iota(jnp.int32, (WIDTH, WIDTH), 1)
    table_of_stats = jnp.zeros((WIDTH, WIDTH), F32)
    for tile in range(tiles):
        rows = slice(tile * TILE, (tile + 1) * TILE)
        query2 = split_heads(queries[rows, :])
        key_rows = listed(table, fetched, tile, list_length, 0)
        value_rows = listed(table, fetched, tile, list_length, 1)
        scores = tile_scores(table, query2, key_rows, tile, scale)
        top = jnp.max(scores, axis=1, keepdims=True)
        log_total = top + jnp.log(jnp.sum(jnp.exp(scores - top), axis=1, keepdims=True))
        weights = jnp.exp(scores - log_total).astype(BF16)
        attended = join_heads(dot(weights, value_rows)).astype(BF16)
        attention[rows, :] = attended
        product = grads[rows, :].astype(F32) * attended.astype(F32)
        delta = jnp.sum(split_heads(product), axis=1, keepdims=True)
        table_of_stats = jnp.where(lane == tile, log_total, table_of_stats)
        table_of_stats = jnp.where(lane == tiles + tile, delta, table_of_stats)
    stats[...] = table_of_stats
    by_row = table_of_stats.T
    row = lax.broadcasted_iota(jnp.int32, (STAT_ROWS, WIDTH), 0)
    for tile in range(tiles):
        block = jnp.zeros((STAT_ROWS, WIDTH), F32)
        for at, value in ((0, by_row[tile : tile + 1]), (3, by_row[tiles + tile : tiles + tile + 1])):
            for part in range(3):
                rounded = value.astype(BF16).astype(F32)
                block = jnp.where(row == at + part, rounded, block)
                value = value - rounded
        spread[tile, 0:TILE, :] = grads[tile * TILE : (tile + 1) * TILE, :]
        spread[tile, TILE : TILE + STAT_ROWS, :] = block.astype(BF16)

    for i in range(seq_count):
        staged[i, chunk : chunk + TILE + STAT_ROWS, :] = spread[table[3, i]]
    attention_t = attention[...].astype(F32).T.astype(BF16)
    across = seq_count * FEW // WIDTH
    steps = GATHERED // 4
    stores = []
    for at in range(steps):
        rows = jnp.concatenate([joined(core[0], own, other, 2 * at + k) for k in range(2)], axis=0)
        part = dot_nt(attention_t, rows)
        run = at * across // steps
        first = (at - run * steps // across) * rows.shape[0] // WIDTH * FEW
        for down in range(WIDTH // FEW):
            lines = part[down * FEW : (down + 1) * FEW, :]
            for k in range(0, rows.shape[0], 2 * WIDTH):
                pair = jnp.concatenate([lines[:, k : k + WIDTH], lines[:, k + WIDTH : k + 2 * WIDTH]], axis=0)
                start = first + k // WIDTH * FEW
                staged[down * across + run, start : start + 2 * FEW, :] = pair.astype(BF16)
        if (at + 1) * across % steps == 0:
            for down in range(WIDTH // FEW):
                c = down * across + run
                stores.append(pltpu.make_async_copy(staged.at[c], out.at[c], sems.at[c]))
                stores[-1].start()
    for store in stores:
        store.wait()
    asked.wait()


def query_kernel(scale, list_length, table, fetched, queries, grads, stats, out):
    tiles = queries.shape[0] // TILE
    for tile in range(tiles):
        rows = slice(tile * TILE, (tile + 1) * TILE)
        key_rows = listed(table, fetched, tile, list_length, 0)
        value_rows = listed(table, fetched, tile, list_length, 1)
        scores = tile_scores(table, split_heads(queries[rows, :]), key_rows, tile, scale)
        probs = jnp.exp(scores - stats[:, tile : tile + 1])
        grad_probs = dot_nt(split_heads(grads[rows, :]), value_rows)
        grad_scores = (probs * (grad_probs - stats[:, tiles + tile : tiles + tile + 1])).astype(BF16)
        out[rows, :] = (join_heads(dot(grad_scores, key_rows)) * scale).astype(BF16)


def sum_kernel(chunk, arrived, mixed_part, grad_queries, out, total_of, sems):
    total = arrived[0, 0:chunk, :].astype(F32)
    for i in range(1, arrived.shape[0]):
        total += arrived[i, 0:chunk, :].astype(F32)
    total = total.astype(BF16)
    copies = total_of.shape[0]
    for i in range(copies):
        total_of[i] = total
    stores = []
    for at in range(out.shape[0] // copies):
        stores.append(pltpu.make_async_copy(total_of, out.at[pl.ds(at * copies, copies)], sems.at[at]))
        stores[-1].start()
    for store in stores:
        store.wait()


def owner_kernel(scale, chunk, group, table, requests, arrived, keys, values, grad_keys, grad_values, key_sum, value_sum):
    tok_rows = keys.shape[0]
    senders = arrived.shape[0]
    key_tile = lax.broadcasted_iota(jnp.int32, (tok_rows, WIDTH), 0) // TILE
    key_sum[...] = jnp.zeros_like(key_sum)
    value_sum[...] = jnp.zeros_like(value_sum)

    def step(at, carry):
        query2, grad2, logs, deltas, keeps = [], [], [], [], []
        for k in range(group):
            i = at * group + k
            query2.append(split_heads(requests[i]))
            grad2.append(split_heads(arrived[i, chunk : chunk + TILE, :]))
            parts = arrived[i, chunk + TILE : chunk + TILE + STAT_ROWS, :].astype(F32)
            logs.append(parts[0:1] + parts[1:2] + parts[2:3])
            deltas.append(parts[3:4] + parts[4:5] + parts[5:6])
            wanted = jnp.where(table[1, i] > 0, table[0, i], -1)
            keeps.append(key_tile == wanted)
        query2 = jnp.concatenate(query2, axis=0)
        grad2 = jnp.concatenate(grad2, axis=0)
        log_total = jnp.concatenate(logs, axis=1)
        delta = jnp.concatenate(deltas, axis=1)
        scores = dot_nt(keys[...], query2) * scale
        gaps = scores - log_total
        gaps = jnp.concatenate(
            [
                jnp.where(keeps[k], gaps[:, k * WIDTH : (k + 1) * WIDTH], -jnp.inf)
                for k in range(group)
            ],
            axis=1,
        )
        probs = jnp.exp(gaps)
        grad_probs = dot_nt(values[...], grad2)
        grad_scores = (probs * (grad_probs - delta)).astype(BF16)
        key_sum[...] += dot(grad_scores, query2)
        value_sum[...] += dot(probs.astype(BF16), grad2)
        return carry

    lax.fori_loop(0, senders // group, step, 0)
    grad_keys[...] = (key_sum[...] * scale).astype(BF16)
    grad_values[...] = value_sum[...].astype(BF16)


def write_kernel(gathered, out, sem):
    copy = pltpu.make_async_copy(gathered, out, sem)
    copy.start()
    copy.wait()


def exchange(blocks):
    return lax.all_to_all(blocks, "seq", split_axis=0, concat_axis=0, tiled=True)


def swap_cores(array):
    return lax.ppermute(array, "core", [(0, 1), (1, 0)])


def to_chip(array, apart):
    chips = lax.axis_size("z")
    return lax.ppermute(array, "z", [(z, (z + apart) % chips) for z in range(chips)])


def body(queries, keys, values, out_weight, grad_mixed, kv_tiles, kv_counts):
    tok_rows, row_width = queries.shape
    tiles_dev = tok_rows // TILE
    list_length = kv_tiles.shape[1]
    seq_count = lax.axis_size("seq")
    scale = 1.0 / math.sqrt(HD)
    model = out_weight.shape[1]
    chunk = model // seq_count
    device = lax.axis_index("seq")
    block = jax.ShapeDtypeStruct((tok_rows, row_width), BF16)

    grad_t = lax.all_gather(grad_mixed.T, "z", axis=0, tiled=True)
    lists = kv_tiles.T
    groups = 4
    outgoing, table = pl.pallas_call(
        pack_kernel,
        out_shape=(
            pltpu.HBM((seq_count, 3 * TILE, row_width), BF16),
            jax.ShapeDtypeStruct((5, seq_count), jnp.int32),
        ),
        in_specs=[SMEM, HBM, HBM, HBM, HBM, HBM],
        out_specs=(HBM, SMEM),
        scratch_shapes=[
            pltpu.SMEM(lists.shape, jnp.int32),
            pltpu.SMEM((1,) + kv_counts.shape, jnp.int32),
            pltpu.VMEM(lists.shape, jnp.int32),
            pltpu.VMEM((1,) + kv_counts.shape, jnp.int32),
            pltpu.VMEM((seq_count, 2 * TILE, row_width), BF16),
            pltpu.VMEM((seq_count, TILE, row_width), BF16),
            pltpu.VMEM(lists.shape, jnp.int32),
            pltpu.SMEM(lists.shape, jnp.int32),
            pltpu.VMEM((3, tok_rows, row_width), BF16),
            pltpu.SemaphoreType.DMA((9 + groups,)),
        ],
        compiler_params=PARAMS,
        name="pack",
    )(
        device[None].astype(jnp.int32),
        stay(lists),
        stay(kv_counts[None, :]),
        stay(queries),
        stay(keys),
        stay(values),
    )
    fetched = exchange(outgoing)
    other_t = swap_cores(grad_t)
    core = lax.axis_index("core")[None].astype(jnp.int32)

    grads = pl.pallas_call(
        grad_kernel,
        out_shape=block,
        in_specs=[SMEM, VMEM, VMEM, HBM],
        out_specs=VMEM,
        scratch_shapes=[pltpu.VMEM(out_weight.shape, BF16), pltpu.SemaphoreType.DMA],
        compiler_params=PARAMS,
        cost_estimate=pl.CostEstimate(flops=3_000_000_000, bytes_accessed=3_000_000, transcendentals=0),
        name="attention_grad",
    )(core, grad_t, other_t, stay(out_weight))

    second, attention, stats, requests = pl.pallas_call(
        functools.partial(forward_kernel, scale, list_length),
        out_shape=(
            pltpu.HBM((seq_count, chunk + TILE + STAT_ROWS, row_width), BF16),
            block,
            jax.ShapeDtypeStruct((WIDTH, WIDTH), F32),
            pltpu.HBM((seq_count, TILE, row_width), BF16),
        ),
        in_specs=[SMEM, VMEM, VMEM, SMEM, VMEM, VMEM, VMEM],
        out_specs=(HBM, VMEM, VMEM, HBM),
        scratch_shapes=[
            pltpu.VMEM((tiles_dev, TILE + STAT_ROWS, row_width), BF16),
            pltpu.VMEM((seq_count, chunk + TILE + STAT_ROWS, row_width), BF16),
            pltpu.SemaphoreType.DMA((seq_count + 1,)),
        ],
        compiler_params=PARAMS,
        name="forward",
    )(table, fetched, queries, core, grad_t, other_t, grads)
    arrived = exchange(second)

    run = grad_mixed.shape[1]
    blocks = model // run // 2
    shares = jax.ShapeDtypeStruct((blocks, run, tok_rows), BF16)
    mine, sent = pl.pallas_call(
        mixed_kernel,
        out_shape=(shares, shares),
        in_specs=[SMEM, HBM, VMEM],
        out_specs=(VMEM, VMEM),
        scratch_shapes=[pltpu.VMEM(out_weight.shape, BF16), pltpu.SemaphoreType.DMA],
        compiler_params=PARAMS,
        name="mixed_share",
    )(core, stay(out_weight), attention)
    mine, *sent = pl.pallas_call(
        pair_kernel,
        out_shape=(
            jax.ShapeDtypeStruct((2, run, tok_rows), F32),
            jax.ShapeDtypeStruct((2, run, tok_rows), BF16),
            jax.ShapeDtypeStruct((2, run, tok_rows), BF16),
            jax.ShapeDtypeStruct((1, run, tok_rows), BF16),
            jax.ShapeDtypeStruct((1, run, tok_rows), BF16),
        ),
        in_specs=[SMEM, VMEM, VMEM],
        out_specs=(VMEM,) * 5,
        compiler_params=PARAMS,
        name="mixed_pair",
    )(lax.axis_index("z")[None].astype(jnp.int32), mine, swap_cores(sent))
    mine, sent = pl.pallas_call(
        near_kernel,
        out_shape=(
            jax.ShapeDtypeStruct((run, tok_rows), F32),
            jax.ShapeDtypeStruct((run, tok_rows), BF16),
        ),
        in_specs=[VMEM] * 5,
        out_specs=(VMEM, VMEM),
        compiler_params=PARAMS,
        name="mixed_near",
    )(mine, *(to_chip(part, apart) for part, apart in zip(sent, (1, -1, 2, -2), strict=True)))

    grad_queries = pl.pallas_call(
        functools.partial(query_kernel, scale, list_length),
        out_shape=block,
        in_specs=[SMEM, VMEM, VMEM, VMEM, VMEM],
        out_specs=VMEM,
        compiler_params=PARAMS,
        cost_estimate=pl.CostEstimate(flops=400_000_000, bytes_accessed=4_000_000, transcendentals=300_000),
        name="query_grad",
    )(table, fetched, queries, grads, stats)

    third = pl.pallas_call(
        functools.partial(sum_kernel, chunk),
        out_shape=pltpu.HBM((seq_count, chunk, row_width), BF16),
        in_specs=[VMEM, ANY, HBM],
        out_specs=HBM,
        scratch_shapes=[pltpu.VMEM((4, chunk, row_width), BF16), pltpu.SemaphoreType.DMA((seq_count // 4,))],
        compiler_params=PARAMS,
        name="sum_share",
    )(arrived, sent, stay(grad_queries))
    gathered = exchange(third)

    grad_keys, grad_values = pl.pallas_call(
        functools.partial(owner_kernel, scale, chunk, 4),
        out_shape=(block, block),
        in_specs=[SMEM, VMEM, VMEM, VMEM, VMEM],
        out_specs=(VMEM, VMEM),
        scratch_shapes=[pltpu.VMEM((tok_rows, row_width), F32), pltpu.VMEM((tok_rows, row_width), F32)],
        compiler_params=PARAMS,
        cost_estimate=pl.CostEstimate(flops=1_100_000_000, bytes_accessed=4_000_000, transcendentals=1_000_000),
        name="owner_grad",
    )(table, requests, arrived, keys, values)
    mixed = pl.pallas_call(
        last_kernel,
        out_shape=jax.ShapeDtypeStruct((run, tok_rows), BF16),
        in_specs=[VMEM, VMEM, HBM],
        out_specs=VMEM,
        compiler_params=PARAMS,
        name="mixed_last",
    )(mine, to_chip(sent, 4), stay(grad_keys)).T
    written = pl.pallas_call(
        write_kernel,
        out_shape=pltpu.HBM(gathered.shape, BF16),
        in_specs=[VMEM],
        out_specs=HBM,
        scratch_shapes=[pltpu.SemaphoreType.DMA],
        compiler_params=PARAMS,
        name="write",
    )(pltpu.with_memory_space_constraint(gathered, pltpu.VMEM))
    weight_grad = (
        written.reshape(row_width // FEW, seq_count * FEW // row_width, chunk // FEW, FEW, WIDTH)
        .transpose(0, 3, 1, 2, 4)
        .reshape(out_weight.shape)
    )
    return (mixed, grad_queries, grad_keys, grad_values, weight_grad)


def solution(mesh):
    seq_count, head_count = mesh.devices.shape
    split = Mesh(mesh.devices.reshape(seq_count, head_count // 2, 2), ("seq", "z", "core"))
    both = P("seq", ("z", "core"))
    rows = P(("z", "core"), None)
    return jax.shard_map(
        body,
        mesh=split,
        in_specs=(both, both, both, rows, both, P(), P()),
        out_specs=(both, both, both, both, rows),
        check_vma=False,
    )
```

```python
import functools
import math

import jax
import jax.numpy as jnp
from jax import lax
from jax.experimental import pallas as pl
from jax.experimental.pallas import tpu as pltpu
from jax.sharding import Mesh, PartitionSpec as P

TILE = 64
HD = 64
WIDTH = 2 * HD
STAT_ROWS = 8
FEW = 8
GATHERED = 16
BF16 = jnp.bfloat16
F32 = jnp.float32
VMEM = pl.BlockSpec(memory_space=pltpu.VMEM)
SMEM = pl.BlockSpec(memory_space=pltpu.SMEM)
HBM = pl.BlockSpec(memory_space=pltpu.HBM)
ANY = pl.BlockSpec(memory_space=pl.ANY)
PARAMS = pltpu.CompilerParams(vmem_limit_bytes=16 * 1024 * 1024)
NT = (((1,), (1,)), ((), ()))


def stay(array):
    return pltpu.with_memory_space_constraint(array, pltpu.HBM)


def dot(a, b):
    return jnp.dot(a, b, preferred_element_type=F32)


def dot_nt(a, b):
    return lax.dot_general(a, b, NT, preferred_element_type=F32)


def split_heads(rows):
    lane = lax.broadcasted_iota(jnp.int32, rows.shape, 1)
    zero = jnp.zeros_like(rows)
    return jnp.concatenate(
        [jnp.where(lane < HD, rows, zero), jnp.where(lane < HD, zero, rows)], axis=0
    )


def join_heads(rows):
    half = rows.shape[0] // 2
    lane = lax.broadcasted_iota(jnp.int32, (half, rows.shape[1]), 1)
    return jnp.where(lane < HD, rows[:half], rows[half:])


def pack_kernel(
    place, lists_h, counts_h, queries, keys, values, out, table,
    lists, counts, lists_v, counts_v, staged, asking, codes_v, codes, held, sems,
):
    list_length, tile_count = lists_v.shape
    seq_count = out.shape[0]
    tiles = tile_count // seq_count
    device = place[0]
    pairs = (
        (lists_h, lists_v), (counts_h, counts_v), (lists_h, lists), (counts_h, counts),
        (keys, held.at[0]), (values, held.at[1]), (queries, held.at[2]),
    )
    loads = [pltpu.make_async_copy(*pair, sems.at[k]) for k, pair in enumerate(pairs)]
    for load in loads:
        load.start()
    for load in loads[:2]:
        load.wait()
    listed_tile = lists_v[...]
    entry = lax.broadcasted_iota(jnp.int32, listed_tile.shape, 0)
    code = lax.rem(listed_tile, tiles) + jnp.where(entry < counts_v[...], tiles, 0)
    code = jnp.where(lax.div(listed_tile, tiles) == device, code, 0)
    code = jnp.broadcast_to(jnp.sum(code, axis=0, keepdims=True), code.shape)
    codes_v[...] = sum(
        (pltpu.roll(code, tile_count - tile, 1) for tile in range(1, tiles)), start=code
    )
    scalars = pltpu.make_async_copy(codes_v, codes, sems.at[7])
    scalars.start()
    for load in loads[2:4]:
        load.wait()
    for tile in range(tiles):
        table[4, tile] = counts[0, device * tiles + tile]
        for j in range(list_length):
            owner = lax.div(lists[j, device * tiles + tile], tiles)
            table[2, tile * list_length + j] = owner
            table[3, owner] = tile
    groups = sems.shape[0] - 9
    each = seq_count // groups
    loads[6].wait()
    for i in range(seq_count):
        mine = pl.ds(pl.multiple_of(table[3, i] * TILE, TILE), TILE)
        asking[i] = held[2, mine, :]
    stores = [pltpu.make_async_copy(asking, out.at[:, pl.ds(2 * TILE, TILE), :], sems.at[8])]
    stores[0].start()
    scalars.wait()
    for load in loads[4:6]:
        load.wait()
    for group in range(groups):
        span = pl.ds(group * each, each)
        for i in range(group * each, (group + 1) * each):
            code = codes[0, i * tiles]
            asked = lax.rem(code, tiles)
            table[0, i] = asked
            table[1, i] = lax.div(code, tiles)
            tile = pl.ds(pl.multiple_of(asked * TILE, TILE), TILE)
            staged[i, 0:TILE, :] = held[0, tile, :]
            staged[i, TILE : 2 * TILE, :] = held[1, tile, :]
        stores.append(
            pltpu.make_async_copy(staged.at[span], out.at[span, pl.ds(0, 2 * TILE), :], sems.at[9 + group])
        )
        stores[-1].start()
    for store in stores:
        store.wait()


def joined(core, own, other, z):
    run = 2 * own.shape[0] // GATHERED
    mine, theirs = own[z * run : (z + 1) * run, :], other[z * run : (z + 1) * run, :]
    first = core == 0
    return jnp.concatenate([jnp.where(first, mine, theirs), jnp.where(first, theirs, mine)], axis=0)


def partial_grad(core, weight, mine, theirs):
    none = jnp.zeros_like(mine if theirs is None else theirs)
    own, other = (none if half is None else half for half in (mine, theirs))
    wide = 2 * weight.shape[1] // GATHERED
    return sum(
        dot(weight[:, z * wide : (z + 1) * wide], joined(core, own, other, z)) for z in range(GATHERED // 2)
    )


def own_grad_kernel(core, own, weight_h, partial, weight, sem):
    load = pltpu.make_async_copy(weight_h, weight, sem)
    load.start()
    load.wait()
    partial[...] = partial_grad(core[0], weight, own[...], None)


def other_grad_kernel(core, other, weight, partial, grads):
    grads[...] = (partial[...] + partial_grad(core[0], weight, None, other[...])).T.astype(BF16)


def mixed_kernel(core, weight_h, attention, keep, send, weight, sem):
    load = pltpu.make_async_copy(weight_h, weight, sem)
    load.start()
    load.wait()
    chips, run = keep.shape[0], keep.shape[1]
    weight_t = weight[...].T
    first_core = core[0] == 0
    for z in range(chips):
        shares = [
            dot_nt(weight_t[(2 * z + k) * run : (2 * z + k + 1) * run], attention[...]).astype(BF16)
            for k in range(2)
        ]
        keep[z] = jnp.where(first_core, shares[0], shares[1])
        send[z] = jnp.where(first_core, shares[1], shares[0])


def pair_kernel(place, mine, arrived, keep, next_1, back_1, next_2, back_2):
    chips = mine.shape[0]
    homes = {
        0: (keep, 0), 4: (keep, 1), 1: (next_1, 0), 5: (next_1, 1),
        7: (back_1, 0), 3: (back_1, 1), 2: (next_2, 0), 6: (back_2, 0),
    }
    for z in range(chips):
        total = mine[z].astype(F32) + arrived[z].astype(F32)
        apart = lax.rem(z + chips - place[0], chips)
        for distance, (target, slot) in homes.items():

            @pl.when(apart == distance)
            def _(target=target, slot=slot):
                target[slot] = total.astype(target.dtype)


def near_kernel(mine, next_1, back_1, next_2, keep, send):
    here, opposite = (mine[i] + next_1[i].astype(F32) + back_1[i].astype(F32) for i in range(2))
    keep[...] = here + next_2[0].astype(F32)
    send[...] = opposite.astype(BF16)


def last_kernel(mine, back_2, arrived, grad_keys, out):
    total = mine[...] + back_2[0].astype(F32)
    out[...] = (total + arrived[...].astype(F32)).astype(BF16)


def listed(table, fetched, tile, list_length, part):
    return jnp.concatenate(
        [
            fetched[table[2, tile * list_length + j], part * TILE : (part + 1) * TILE, :]
            for j in range(list_length)
        ],
        axis=0,
    )


def tile_scores(table, query2, key_rows, tile, scale):
    scores = dot_nt(query2, key_rows) * scale
    column = lax.broadcasted_iota(jnp.int32, scores.shape, 1)
    return jnp.where(column < table[4, tile] * TILE, scores, -jnp.inf)


def forward_kernel(
    scale, list_length, table, fetched, queries, core, own, other, grads, out, attention, stats, requests,
    spread, staged, sems,
):
    tiles = queries.shape[0] // TILE
    seq_count = out.shape[0]
    asked = pltpu.make_async_copy(fetched.at[:, pl.ds(2 * TILE, TILE), :], requests, sems.at[seq_count])
    asked.start()
    model = 2 * own.shape[0]
    chunk = model // seq_count
    lane = lax.broadcasted_iota(jnp.int32, (WIDTH, WIDTH), 1)
    table_of_stats = jnp.zeros((WIDTH, WIDTH), F32)
    for tile in range(tiles):
        rows = slice(tile * TILE, (tile + 1) * TILE)
        query2 = split_heads(queries[rows, :])
        key_rows = listed(table, fetched, tile, list_length, 0)
        value_rows = listed(table, fetched, tile, list_length, 1)
        scores = tile_scores(table, query2, key_rows, tile, scale)
        top = jnp.max(scores, axis=1, keepdims=True)
        log_total = top + jnp.log(jnp.sum(jnp.exp(scores - top), axis=1, keepdims=True))
        weights = jnp.exp(scores - log_total).astype(BF16)
        attended = join_heads(dot(weights, value_rows)).astype(BF16)
        attention[rows, :] = attended
        product = grads[rows, :].astype(F32) * attended.astype(F32)
        delta = jnp.sum(split_heads(product), axis=1, keepdims=True)
        table_of_stats = jnp.where(lane == tile, log_total, table_of_stats)
        table_of_stats = jnp.where(lane == tiles + tile, delta, table_of_stats)
    stats[...] = table_of_stats
    by_row = table_of_stats.T
    row = lax.broadcasted_iota(jnp.int32, (STAT_ROWS, WIDTH), 0)
    for tile in range(tiles):
        block = jnp.zeros((STAT_ROWS, WIDTH), F32)
        for at, value in ((0, by_row[tile : tile + 1]), (3, by_row[tiles + tile : tiles + tile + 1])):
            for part in range(3):
                rounded = value.astype(BF16).astype(F32)
                block = jnp.where(row == at + part, rounded, block)
                value = value - rounded
        spread[tile, 0:TILE, :] = grads[tile * TILE : (tile + 1) * TILE, :]
        spread[tile, TILE : TILE + STAT_ROWS, :] = block.astype(BF16)

    for i in range(seq_count):
        staged[i, chunk : chunk + TILE + STAT_ROWS, :] = spread[table[3, i]]
    attention_t = attention[...].astype(F32).T.astype(BF16)
    across = seq_count * FEW // WIDTH
    steps = GATHERED // 4
    stores = []
    for at in range(steps):
        rows = jnp.concatenate([joined(core[0], own, other, 2 * at + k) for k in range(2)], axis=0)
        part = dot_nt(attention_t, rows)
        run = at * across // steps
        first = (at - run * steps // across) * rows.shape[0] // WIDTH * FEW
        for down in range(WIDTH // FEW):
            lines = part[down * FEW : (down + 1) * FEW, :]
            for k in range(0, rows.shape[0], 2 * WIDTH):
                pair = jnp.concatenate([lines[:, k : k + WIDTH], lines[:, k + WIDTH : k + 2 * WIDTH]], axis=0)
                start = first + k // WIDTH * FEW
                staged[down * across + run, start : start + 2 * FEW, :] = pair.astype(BF16)
        if (at + 1) * across % steps == 0:
            for down in range(WIDTH // FEW):
                c = down * across + run
                stores.append(pltpu.make_async_copy(staged.at[c], out.at[c], sems.at[c]))
                stores[-1].start()
    for store in stores:
        store.wait()
    asked.wait()


def query_kernel(scale, list_length, table, fetched, queries, grads, stats, out):
    tiles = queries.shape[0] // TILE
    for tile in range(tiles):
        rows = slice(tile * TILE, (tile + 1) * TILE)
        key_rows = listed(table, fetched, tile, list_length, 0)
        value_rows = listed(table, fetched, tile, list_length, 1)
        scores = tile_scores(table, split_heads(queries[rows, :]), key_rows, tile, scale)
        probs = jnp.exp(scores - stats[:, tile : tile + 1])
        grad_probs = dot_nt(split_heads(grads[rows, :]), value_rows)
        grad_scores = (probs * (grad_probs - stats[:, tiles + tile : tiles + tile + 1])).astype(BF16)
        out[rows, :] = (join_heads(dot(grad_scores, key_rows)) * scale).astype(BF16)


def sum_kernel(chunk, arrived, mixed_part, grad_queries, out, total_of, sems):
    total = arrived[0, 0:chunk, :].astype(F32)
    for i in range(1, arrived.shape[0]):
        total += arrived[i, 0:chunk, :].astype(F32)
    total = total.astype(BF16)
    copies = total_of.shape[0]
    for i in range(copies):
        total_of[i] = total
    stores = []
    for at in range(out.shape[0] // copies):
        stores.append(pltpu.make_async_copy(total_of, out.at[pl.ds(at * copies, copies)], sems.at[at]))
        stores[-1].start()
    for store in stores:
        store.wait()


def owner_kernel(scale, chunk, group, table, requests, arrived, keys, values, grad_keys, grad_values, key_sum, value_sum):
    tok_rows = keys.shape[0]
    senders = arrived.shape[0]
    key_tile = lax.broadcasted_iota(jnp.int32, (tok_rows, WIDTH), 0) // TILE
    key_sum[...] = jnp.zeros_like(key_sum)
    value_sum[...] = jnp.zeros_like(value_sum)

    def step(at, carry):
        query2, grad2, logs, deltas, keeps = [], [], [], [], []
        for k in range(group):
            i = at * group + k
            query2.append(split_heads(requests[i]))
            grad2.append(split_heads(arrived[i, chunk : chunk + TILE, :]))
            parts = arrived[i, chunk + TILE : chunk + TILE + STAT_ROWS, :].astype(F32)
            logs.append(parts[0:1] + parts[1:2] + parts[2:3])
            deltas.append(parts[3:4] + parts[4:5] + parts[5:6])
            wanted = jnp.where(table[1, i] > 0, table[0, i], -1)
            keeps.append(key_tile == wanted)
        query2 = jnp.concatenate(query2, axis=0)
        grad2 = jnp.concatenate(grad2, axis=0)
        log_total = jnp.concatenate(logs, axis=1)
        delta = jnp.concatenate(deltas, axis=1)
        scores = dot_nt(keys[...], query2) * scale
        gaps = scores - log_total
        gaps = jnp.concatenate(
            [
                jnp.where(keeps[k], gaps[:, k * WIDTH : (k + 1) * WIDTH], -jnp.inf)
                for k in range(group)
            ],
            axis=1,
        )
        probs = jnp.exp(gaps)
        grad_probs = dot_nt(values[...], grad2)
        grad_scores = (probs * (grad_probs - delta)).astype(BF16)
        key_sum[...] += dot(grad_scores, query2)
        value_sum[...] += dot(probs.astype(BF16), grad2)
        return carry

    lax.fori_loop(0, senders // group, step, 0)
    grad_keys[...] = (key_sum[...] * scale).astype(BF16)
    grad_values[...] = value_sum[...].astype(BF16)


def write_kernel(gathered, out, sem):
    copy = pltpu.make_async_copy(gathered, out, sem)
    copy.start()
    copy.wait()


def exchange(blocks):
    return lax.all_to_all(blocks, "seq", split_axis=0, concat_axis=0, tiled=True)


def swap_cores(array):
    return lax.ppermute(array, "core", [(0, 1), (1, 0)])


def to_chip(array, apart):
    chips = lax.axis_size("z")
    return lax.ppermute(array, "z", [(z, (z + apart) % chips) for z in range(chips)])


def body(queries, keys, values, out_weight, grad_mixed, kv_tiles, kv_counts):
    tok_rows, row_width = queries.shape
    tiles_dev = tok_rows // TILE
    list_length = kv_tiles.shape[1]
    seq_count = lax.axis_size("seq")
    scale = 1.0 / math.sqrt(HD)
    model = out_weight.shape[1]
    chunk = model // seq_count
    device = lax.axis_index("seq")
    block = jax.ShapeDtypeStruct((tok_rows, row_width), BF16)

    grad_t = lax.all_gather(grad_mixed.T, "z", axis=0, tiled=True)
    lists = kv_tiles.T
    groups = 4
    outgoing, table = pl.pallas_call(
        pack_kernel,
        out_shape=(
            pltpu.HBM((seq_count, 3 * TILE, row_width), BF16),
            jax.ShapeDtypeStruct((5, seq_count), jnp.int32),
        ),
        in_specs=[SMEM, HBM, HBM, HBM, HBM, HBM],
        out_specs=(HBM, SMEM),
        scratch_shapes=[
            pltpu.SMEM(lists.shape, jnp.int32),
            pltpu.SMEM((1,) + kv_counts.shape, jnp.int32),
            pltpu.VMEM(lists.shape, jnp.int32),
            pltpu.VMEM((1,) + kv_counts.shape, jnp.int32),
            pltpu.VMEM((seq_count, 2 * TILE, row_width), BF16),
            pltpu.VMEM((seq_count, TILE, row_width), BF16),
            pltpu.VMEM(lists.shape, jnp.int32),
            pltpu.SMEM(lists.shape, jnp.int32),
            pltpu.VMEM((3, tok_rows, row_width), BF16),
            pltpu.SemaphoreType.DMA((9 + groups,)),
        ],
        compiler_params=PARAMS,
        name="pack",
    )(
        device[None].astype(jnp.int32),
        stay(lists),
        stay(kv_counts[None, :]),
        stay(queries),
        stay(keys),
        stay(values),
    )
    fetched = exchange(outgoing)
    other_t = swap_cores(grad_t)
    core = lax.axis_index("core")[None].astype(jnp.int32)

    partial, weight_v = pl.pallas_call(
        own_grad_kernel,
        out_shape=(
            jax.ShapeDtypeStruct((row_width, tok_rows), F32),
            jax.ShapeDtypeStruct(out_weight.shape, BF16),
        ),
        in_specs=[SMEM, VMEM, HBM],
        out_specs=(VMEM, VMEM),
        scratch_shapes=[pltpu.SemaphoreType.DMA],
        compiler_params=PARAMS,
        cost_estimate=pl.CostEstimate(flops=3_000_000_000, bytes_accessed=3_000_000, transcendentals=0),
        name="own_grad",
    )(core, grad_t, stay(out_weight))
    grads = pl.pallas_call(
        other_grad_kernel,
        out_shape=block,
        in_specs=[SMEM, VMEM, VMEM, VMEM],
        out_specs=VMEM,
        compiler_params=PARAMS,
        name="other_grad",
    )(core, other_t, weight_v, partial)

    second, attention, stats, requests = pl.pallas_call(
        functools.partial(forward_kernel, scale, list_length),
        out_shape=(
            pltpu.HBM((seq_count, chunk + TILE + STAT_ROWS, row_width), BF16),
            block,
            jax.ShapeDtypeStruct((WIDTH, WIDTH), F32),
            pltpu.HBM((seq_count, TILE, row_width), BF16),
        ),
        in_specs=[SMEM, VMEM, VMEM, SMEM, VMEM, VMEM, VMEM],
        out_specs=(HBM, VMEM, VMEM, HBM),
        scratch_shapes=[
            pltpu.VMEM((tiles_dev, TILE + STAT_ROWS, row_width), BF16),
            pltpu.VMEM((seq_count, chunk + TILE + STAT_ROWS, row_width), BF16),
            pltpu.SemaphoreType.DMA((seq_count + 1,)),
        ],
        compiler_params=PARAMS,
        name="forward",
    )(table, fetched, queries, core, grad_t, other_t, grads)
    arrived = exchange(second)

    run = grad_mixed.shape[1]
    blocks = model // run // 2
    shares = jax.ShapeDtypeStruct((blocks, run, tok_rows), BF16)
    mine, sent = pl.pallas_call(
        mixed_kernel,
        out_shape=(shares, shares),
        in_specs=[SMEM, HBM, VMEM],
        out_specs=(VMEM, VMEM),
        scratch_shapes=[pltpu.VMEM(out_weight.shape, BF16), pltpu.SemaphoreType.DMA],
        compiler_params=PARAMS,
        name="mixed_share",
    )(core, stay(out_weight), attention)
    mine, next_1, back_1, next_2, back_2 = pl.pallas_call(
        pair_kernel,
        out_shape=(
            jax.ShapeDtypeStruct((2, run, tok_rows), F32),
            jax.ShapeDtypeStruct((2, run, tok_rows), BF16),
            jax.ShapeDtypeStruct((2, run, tok_rows), BF16),
            jax.ShapeDtypeStruct((1, run, tok_rows), BF16),
            jax.ShapeDtypeStruct((1, run, tok_rows), BF16),
        ),
        in_specs=[SMEM, VMEM, VMEM],
        out_specs=(VMEM,) * 5,
        compiler_params=PARAMS,
        name="mixed_pair",
    )(lax.axis_index("z")[None].astype(jnp.int32), mine, swap_cores(sent))
    mine, sent = pl.pallas_call(
        near_kernel,
        out_shape=(
            jax.ShapeDtypeStruct((run, tok_rows), F32),
            jax.ShapeDtypeStruct((run, tok_rows), BF16),
        ),
        in_specs=[VMEM] * 4,
        out_specs=(VMEM, VMEM),
        compiler_params=PARAMS,
        name="mixed_near",
    )(mine, to_chip(next_1, 1), to_chip(back_1, -1), to_chip(next_2, 2))

    grad_queries = pl.pallas_call(
        functools.partial(query_kernel, scale, list_length),
        out_shape=block,
        in_specs=[SMEM, VMEM, VMEM, VMEM, VMEM],
        out_specs=VMEM,
        compiler_params=PARAMS,
        cost_estimate=pl.CostEstimate(flops=400_000_000, bytes_accessed=4_000_000, transcendentals=300_000),
        name="query_grad",
    )(table, fetched, queries, grads, stats)

    third = pl.pallas_call(
        functools.partial(sum_kernel, chunk),
        out_shape=pltpu.HBM((seq_count, chunk, row_width), BF16),
        in_specs=[VMEM, ANY, HBM],
        out_specs=HBM,
        scratch_shapes=[pltpu.VMEM((4, chunk, row_width), BF16), pltpu.SemaphoreType.DMA((seq_count // 4,))],
        compiler_params=PARAMS,
        name="sum_share",
    )(arrived, sent, stay(grad_queries))
    gathered = exchange(third)

    grad_keys, grad_values = pl.pallas_call(
        functools.partial(owner_kernel, scale, chunk, 4),
        out_shape=(block, block),
        in_specs=[SMEM, VMEM, VMEM, VMEM, VMEM],
        out_specs=(VMEM, VMEM),
        scratch_shapes=[pltpu.VMEM((tok_rows, row_width), F32), pltpu.VMEM((tok_rows, row_width), F32)],
        compiler_params=PARAMS,
        cost_estimate=pl.CostEstimate(flops=1_100_000_000, bytes_accessed=4_000_000, transcendentals=1_000_000),
        name="owner_grad",
    )(table, requests, arrived, keys, values)
    mixed = pl.pallas_call(
        last_kernel,
        out_shape=jax.ShapeDtypeStruct((run, tok_rows), BF16),
        in_specs=[VMEM, VMEM, VMEM, HBM],
        out_specs=VMEM,
        compiler_params=PARAMS,
        name="mixed_last",
    )(mine, to_chip(back_2, -2), to_chip(sent, 4), stay(grad_keys)).T
    written = pl.pallas_call(
        write_kernel,
        out_shape=pltpu.HBM(gathered.shape, BF16),
        in_specs=[VMEM],
        out_specs=HBM,
        scratch_shapes=[pltpu.SemaphoreType.DMA],
        compiler_params=PARAMS,
        name="write",
    )(pltpu.with_memory_space_constraint(gathered, pltpu.VMEM))
    weight_grad = (
        written.reshape(row_width // FEW, seq_count * FEW // row_width, chunk // FEW, FEW, WIDTH)
        .transpose(0, 3, 1, 2, 4)
        .reshape(out_weight.shape)
    )
    return (mixed, grad_queries, grad_keys, grad_values, weight_grad)


def solution(mesh):
    seq_count, head_count = mesh.devices.shape
    split = Mesh(mesh.devices.reshape(seq_count, head_count // 2, 2), ("seq", "z", "core"))
    both = P("seq", ("z", "core"))
    rows = P(("z", "core"), None)
    return jax.shard_map(
        body,
        mesh=split,
        in_specs=(both, both, both, rows, both, P(), P()),
        out_specs=(both, both, both, both, rows),
        check_vma=False,
    )
```

```python
import functools
import math

import jax
import jax.numpy as jnp
from jax import lax
from jax.experimental import pallas as pl
from jax.experimental.pallas import tpu as pltpu
from jax.sharding import Mesh, PartitionSpec as P

TILE = 64
HD = 64
WIDTH = 2 * HD
STAT_ROWS = 8
FEW = 8
GATHERED = 16
BF16 = jnp.bfloat16
F32 = jnp.float32
VMEM = pl.BlockSpec(memory_space=pltpu.VMEM)
SMEM = pl.BlockSpec(memory_space=pltpu.SMEM)
HBM = pl.BlockSpec(memory_space=pltpu.HBM)
ANY = pl.BlockSpec(memory_space=pl.ANY)
PARAMS = pltpu.CompilerParams(vmem_limit_bytes=16 * 1024 * 1024)
NT = (((1,), (1,)), ((), ()))


def stay(array):
    return pltpu.with_memory_space_constraint(array, pltpu.HBM)


def dot(a, b):
    return jnp.dot(a, b, preferred_element_type=F32)


def dot_nt(a, b):
    return lax.dot_general(a, b, NT, preferred_element_type=F32)


def split_heads(rows):
    lane = lax.broadcasted_iota(jnp.int32, rows.shape, 1)
    zero = jnp.zeros_like(rows)
    return jnp.concatenate(
        [jnp.where(lane < HD, rows, zero), jnp.where(lane < HD, zero, rows)], axis=0
    )


def join_heads(rows):
    half = rows.shape[0] // 2
    lane = lax.broadcasted_iota(jnp.int32, (half, rows.shape[1]), 1)
    return jnp.where(lane < HD, rows[:half], rows[half:])


def pack_kernel(
    place, lists_h, counts_h, queries, keys, values, out, table,
    lists, counts, lists_v, counts_v, staged, asking, codes_v, codes, held, sems,
):
    list_length, tile_count = lists_v.shape
    seq_count = out.shape[0]
    tiles = tile_count // seq_count
    device = place[0]
    pairs = (
        (lists_h, lists_v), (counts_h, counts_v), (lists_h, lists), (counts_h, counts),
        (keys, held.at[0]), (values, held.at[1]), (queries, held.at[2]),
    )
    loads = [pltpu.make_async_copy(*pair, sems.at[k]) for k, pair in enumerate(pairs)]
    for load in loads:
        load.start()
    for load in loads[:2]:
        load.wait()
    listed_tile = lists_v[...]
    entry = lax.broadcasted_iota(jnp.int32, listed_tile.shape, 0)
    code = lax.rem(listed_tile, tiles) + jnp.where(entry < counts_v[...], tiles, 0)
    code = jnp.where(lax.div(listed_tile, tiles) == device, code, 0)
    code = jnp.broadcast_to(jnp.sum(code, axis=0, keepdims=True), code.shape)
    codes_v[...] = sum(
        (pltpu.roll(code, tile_count - tile, 1) for tile in range(1, tiles)), start=code
    )
    scalars = pltpu.make_async_copy(codes_v, codes, sems.at[7])
    scalars.start()
    for load in loads[2:4]:
        load.wait()
    for tile in range(tiles):
        table[4, tile] = counts[0, device * tiles + tile]
        for j in range(list_length):
            owner = lax.div(lists[j, device * tiles + tile], tiles)
            table[2, tile * list_length + j] = owner
            table[3, owner] = tile
    groups = sems.shape[0] - 9
    each = seq_count // groups
    loads[6].wait()
    for i in range(seq_count):
        mine = pl.ds(pl.multiple_of(table[3, i] * TILE, TILE), TILE)
        asking[i] = held[2, mine, :]
    stores = [pltpu.make_async_copy(asking, out.at[:, pl.ds(2 * TILE, TILE), :], sems.at[8])]
    stores[0].start()
    scalars.wait()
    for load in loads[4:6]:
        load.wait()
    for group in range(groups):
        span = pl.ds(group * each, each)
        for i in range(group * each, (group + 1) * each):
            code = codes[0, i * tiles]
            asked = lax.rem(code, tiles)
            table[0, i] = asked
            table[1, i] = lax.div(code, tiles)
            tile = pl.ds(pl.multiple_of(asked * TILE, TILE), TILE)
            staged[i, 0:TILE, :] = held[0, tile, :]
            staged[i, TILE : 2 * TILE, :] = held[1, tile, :]
        stores.append(
            pltpu.make_async_copy(staged.at[span], out.at[span, pl.ds(0, 2 * TILE), :], sems.at[9 + group])
        )
        stores[-1].start()
    for store in stores:
        store.wait()


def joined(core, own, other, z):
    run = 2 * own.shape[0] // GATHERED
    mine, theirs = own[z * run : (z + 1) * run, :], other[z * run : (z + 1) * run, :]
    first = core == 0
    return jnp.concatenate([jnp.where(first, mine, theirs), jnp.where(first, theirs, mine)], axis=0)


def partial_grad(core, weight, mine, theirs):
    none = jnp.zeros_like(mine if theirs is None else theirs)
    own, other = (none if half is None else half for half in (mine, theirs))
    wide = 2 * weight.shape[1] // GATHERED
    return sum(
        dot(weight[:, z * wide : (z + 1) * wide], joined(core, own, other, z)) for z in range(GATHERED // 2)
    )


def own_grad_kernel(core, own, weight_h, partial, weight, sem):
    load = pltpu.make_async_copy(weight_h, weight, sem)
    load.start()
    load.wait()
    partial[...] = partial_grad(core[0], weight, own[...], None)


def other_grad_kernel(core, other, weight, partial, grads):
    grads[...] = (partial[...] + partial_grad(core[0], weight, None, other[...])).T.astype(BF16)


def mixed_kernel(core, weight_h, attention, keep, send, weight, sem):
    load = pltpu.make_async_copy(weight_h, weight, sem)
    load.start()
    load.wait()
    chips, run = keep.shape[0], keep.shape[1]
    weight_t = weight[...].T
    first_core = core[0] == 0
    for z in range(chips):
        shares = [
            dot_nt(weight_t[(2 * z + k) * run : (2 * z + k + 1) * run], attention[...]).astype(BF16)
            for k in range(2)
        ]
        keep[z] = jnp.where(first_core, shares[0], shares[1])
        send[z] = jnp.where(first_core, shares[1], shares[0])


def pair_kernel(place, mine, arrived, keep, next_1, back_1, next_2, back_2):
    chips = mine.shape[0]
    homes = {
        0: (keep, 0), 4: (keep, 1), 1: (next_1, 0), 5: (next_1, 1),
        7: (back_1, 0), 3: (back_1, 1), 2: (next_2, 0), 6: (back_2, 0),
    }
    for z in range(chips):
        total = mine[z].astype(F32) + arrived[z].astype(F32)
        apart = lax.rem(z + chips - place[0], chips)
        for distance, (target, slot) in homes.items():

            @pl.when(apart == distance)
            def _(target=target, slot=slot):
                target[slot] = total.astype(target.dtype)


def near_kernel(mine, next_1, back_1, next_2, keep, send):
    here, opposite = (mine[i] + next_1[i].astype(F32) + back_1[i].astype(F32) for i in range(2))
    keep[...] = here + next_2[0].astype(F32)
    send[...] = opposite.astype(BF16)


def last_kernel(mine, back_2, arrived, grad_keys, out):
    total = mine[...] + back_2[0].astype(F32)
    out[...] = (total + arrived[...].astype(F32)).astype(BF16)


def listed(table, fetched, tile, list_length, part):
    return jnp.concatenate(
        [
            fetched[table[2, tile * list_length + j], part * TILE : (part + 1) * TILE, :]
            for j in range(list_length)
        ],
        axis=0,
    )


def tile_scores(table, query2, key_rows, tile, scale):
    scores = dot_nt(query2, key_rows) * scale
    column = lax.broadcasted_iota(jnp.int32, scores.shape, 1)
    return jnp.where(column < table[4, tile] * TILE, scores, -jnp.inf)


def forward_kernel(
    scale, list_length, table, fetched, queries, core, own, other, grads, out, attention, stats,
    spread, staged, sems,
):
    tiles = queries.shape[0] // TILE
    seq_count = out.shape[0]
    model = 2 * own.shape[0]
    chunk = model // seq_count
    lane = lax.broadcasted_iota(jnp.int32, (WIDTH, WIDTH), 1)
    table_of_stats = jnp.zeros((WIDTH, WIDTH), F32)
    for tile in range(tiles):
        rows = slice(tile * TILE, (tile + 1) * TILE)
        query2 = split_heads(queries[rows, :])
        key_rows = listed(table, fetched, tile, list_length, 0)
        value_rows = listed(table, fetched, tile, list_length, 1)
        scores = tile_scores(table, query2, key_rows, tile, scale)
        top = jnp.max(scores, axis=1, keepdims=True)
        log_total = top + jnp.log(jnp.sum(jnp.exp(scores - top), axis=1, keepdims=True))
        weights = jnp.exp(scores - log_total).astype(BF16)
        attended = join_heads(dot(weights, value_rows)).astype(BF16)
        attention[rows, :] = attended
        product = grads[rows, :].astype(F32) * attended.astype(F32)
        delta = jnp.sum(split_heads(product), axis=1, keepdims=True)
        table_of_stats = jnp.where(lane == tile, log_total, table_of_stats)
        table_of_stats = jnp.where(lane == tiles + tile, delta, table_of_stats)
    stats[...] = table_of_stats
    by_row = table_of_stats.T
    row = lax.broadcasted_iota(jnp.int32, (STAT_ROWS, WIDTH), 0)
    for tile in range(tiles):
        block = jnp.zeros((STAT_ROWS, WIDTH), F32)
        for at, value in ((0, by_row[tile : tile + 1]), (3, by_row[tiles + tile : tiles + tile + 1])):
            for part in range(3):
                rounded = value.astype(BF16).astype(F32)
                block = jnp.where(row == at + part, rounded, block)
                value = value - rounded
        spread[tile, 0:TILE, :] = grads[tile * TILE : (tile + 1) * TILE, :]
        spread[tile, TILE : TILE + STAT_ROWS, :] = block.astype(BF16)

    for i in range(seq_count):
        staged[i, chunk : chunk + TILE + STAT_ROWS, :] = spread[table[3, i]]
    attention_t = attention[...].astype(F32).T.astype(BF16)
    across = seq_count * FEW // WIDTH
    steps = GATHERED // 4
    stores = []
    for at in range(steps):
        rows = jnp.concatenate([joined(core[0], own, other, 2 * at + k) for k in range(2)], axis=0)
        part = dot_nt(attention_t, rows)
        run = at * across // steps
        first = (at - run * steps // across) * rows.shape[0] // WIDTH * FEW
        for down in range(WIDTH // FEW):
            lines = part[down * FEW : (down + 1) * FEW, :]
            for k in range(0, rows.shape[0], 2 * WIDTH):
                pair = jnp.concatenate([lines[:, k : k + WIDTH], lines[:, k + WIDTH : k + 2 * WIDTH]], axis=0)
                start = first + k // WIDTH * FEW
                staged[down * across + run, start : start + 2 * FEW, :] = pair.astype(BF16)
        if (at + 1) * across % steps == 0:
            for down in range(WIDTH // FEW):
                c = down * across + run
                stores.append(pltpu.make_async_copy(staged.at[c], out.at[c], sems.at[c]))
                stores[-1].start()
    for store in stores:
        store.wait()


def query_kernel(scale, list_length, table, fetched, queries, grads, stats, out, requests, sem):
    asked = pltpu.make_async_copy(fetched.at[:, pl.ds(2 * TILE, TILE), :], requests, sem)
    asked.start()
    tiles = queries.shape[0] // TILE
    for tile in range(tiles):
        rows = slice(tile * TILE, (tile + 1) * TILE)
        key_rows = listed(table, fetched, tile, list_length, 0)
        value_rows = listed(table, fetched, tile, list_length, 1)
        scores = tile_scores(table, split_heads(queries[rows, :]), key_rows, tile, scale)
        probs = jnp.exp(scores - stats[:, tile : tile + 1])
        grad_probs = dot_nt(split_heads(grads[rows, :]), value_rows)
        grad_scores = (probs * (grad_probs - stats[:, tiles + tile : tiles + tile + 1])).astype(BF16)
        out[rows, :] = (join_heads(dot(grad_scores, key_rows)) * scale).astype(BF16)
    asked.wait()


def sum_kernel(chunk, arrived, mixed_part, grad_queries, out, total_of, sems):
    total = arrived[0, 0:chunk, :].astype(F32)
    for i in range(1, arrived.shape[0]):
        total += arrived[i, 0:chunk, :].astype(F32)
    total = total.astype(BF16)
    copies = total_of.shape[0]
    for i in range(copies):
        total_of[i] = total
    stores = []
    for at in range(out.shape[0] // copies):
        stores.append(pltpu.make_async_copy(total_of, out.at[pl.ds(at * copies, copies)], sems.at[at]))
        stores[-1].start()
    for store in stores:
        store.wait()


def owner_kernel(
    scale, chunk, group, table, requests_h, arrived, keys, values, grad_keys, grad_values,
    key_sum, value_sum, requests, sems,
):
    tok_rows = keys.shape[0]
    senders = arrived.shape[0]
    key_tile = lax.broadcasted_iota(jnp.int32, (tok_rows, WIDTH), 0) // TILE
    loads = [
        pltpu.make_async_copy(
            requests_h.at[pl.ds(at * group, group)], requests.at[pl.ds(at * group, group)], sems.at[at]
        )
        for at in range(senders // group)
    ]
    for load in loads:
        load.start()
    key_sum[...] = jnp.zeros_like(key_sum)
    value_sum[...] = jnp.zeros_like(value_sum)

    def step(at):
        loads[at].wait()
        query2, grad2, logs, deltas, keeps = [], [], [], [], []
        for k in range(group):
            i = at * group + k
            query2.append(split_heads(requests[i]))
            grad2.append(split_heads(arrived[i, chunk : chunk + TILE, :]))
            parts = arrived[i, chunk + TILE : chunk + TILE + STAT_ROWS, :].astype(F32)
            logs.append(parts[0:1] + parts[1:2] + parts[2:3])
            deltas.append(parts[3:4] + parts[4:5] + parts[5:6])
            wanted = jnp.where(table[1, i] > 0, table[0, i], -1)
            keeps.append(key_tile == wanted)
        query2 = jnp.concatenate(query2, axis=0)
        grad2 = jnp.concatenate(grad2, axis=0)
        log_total = jnp.concatenate(logs, axis=1)
        delta = jnp.concatenate(deltas, axis=1)
        scores = dot_nt(keys[...], query2) * scale
        gaps = scores - log_total
        gaps = jnp.concatenate(
            [
                jnp.where(keeps[k], gaps[:, k * WIDTH : (k + 1) * WIDTH], -jnp.inf)
                for k in range(group)
            ],
            axis=1,
        )
        probs = jnp.exp(gaps)
        grad_probs = dot_nt(values[...], grad2)
        grad_scores = (probs * (grad_probs - delta)).astype(BF16)
        key_sum[...] += dot(grad_scores, query2)
        value_sum[...] += dot(probs.astype(BF16), grad2)

    for at in range(senders // group):
        step(at)
    grad_keys[...] = (key_sum[...] * scale).astype(BF16)
    grad_values[...] = value_sum[...].astype(BF16)


def write_kernel(gathered, out, sem):
    copy = pltpu.make_async_copy(gathered, out, sem)
    copy.start()
    copy.wait()


def exchange(blocks):
    return lax.all_to_all(blocks, "seq", split_axis=0, concat_axis=0, tiled=True)


def swap_cores(array):
    return lax.ppermute(array, "core", [(0, 1), (1, 0)])


def to_chip(array, apart):
    chips = lax.axis_size("z")
    return lax.ppermute(array, "z", [(z, (z + apart) % chips) for z in range(chips)])


def body(queries, keys, values, out_weight, grad_mixed, kv_tiles, kv_counts):
    tok_rows, row_width = queries.shape
    tiles_dev = tok_rows // TILE
    list_length = kv_tiles.shape[1]
    seq_count = lax.axis_size("seq")
    scale = 1.0 / math.sqrt(HD)
    model = out_weight.shape[1]
    chunk = model // seq_count
    device = lax.axis_index("seq")
    block = jax.ShapeDtypeStruct((tok_rows, row_width), BF16)

    grad_t = lax.all_gather(grad_mixed.T, "z", axis=0, tiled=True)
    lists = kv_tiles.T
    groups = 4
    outgoing, table = pl.pallas_call(
        pack_kernel,
        out_shape=(
            pltpu.HBM((seq_count, 3 * TILE, row_width), BF16),
            jax.ShapeDtypeStruct((5, seq_count), jnp.int32),
        ),
        in_specs=[SMEM, HBM, HBM, HBM, HBM, HBM],
        out_specs=(HBM, SMEM),
        scratch_shapes=[
            pltpu.SMEM(lists.shape, jnp.int32),
            pltpu.SMEM((1,) + kv_counts.shape, jnp.int32),
            pltpu.VMEM(lists.shape, jnp.int32),
            pltpu.VMEM((1,) + kv_counts.shape, jnp.int32),
            pltpu.VMEM((seq_count, 2 * TILE, row_width), BF16),
            pltpu.VMEM((seq_count, TILE, row_width), BF16),
            pltpu.VMEM(lists.shape, jnp.int32),
            pltpu.SMEM(lists.shape, jnp.int32),
            pltpu.VMEM((3, tok_rows, row_width), BF16),
            pltpu.SemaphoreType.DMA((9 + groups,)),
        ],
        compiler_params=PARAMS,
        name="pack",
    )(
        device[None].astype(jnp.int32),
        stay(lists),
        stay(kv_counts[None, :]),
        stay(queries),
        stay(keys),
        stay(values),
    )
    fetched = exchange(outgoing)
    other_t = swap_cores(grad_t)
    core = lax.axis_index("core")[None].astype(jnp.int32)

    partial, weight_v = pl.pallas_call(
        own_grad_kernel,
        out_shape=(
            jax.ShapeDtypeStruct((row_width, tok_rows), F32),
            jax.ShapeDtypeStruct(out_weight.shape, BF16),
        ),
        in_specs=[SMEM, VMEM, HBM],
        out_specs=(VMEM, VMEM),
        scratch_shapes=[pltpu.SemaphoreType.DMA],
        compiler_params=PARAMS,
        cost_estimate=pl.CostEstimate(flops=3_000_000_000, bytes_accessed=3_000_000, transcendentals=0),
        name="own_grad",
    )(core, grad_t, stay(out_weight))
    grads = pl.pallas_call(
        other_grad_kernel,
        out_shape=block,
        in_specs=[SMEM, VMEM, VMEM, VMEM],
        out_specs=VMEM,
        compiler_params=PARAMS,
        name="other_grad",
    )(core, other_t, weight_v, partial)

    second, attention, stats = pl.pallas_call(
        functools.partial(forward_kernel, scale, list_length),
        out_shape=(
            pltpu.HBM((seq_count, chunk + TILE + STAT_ROWS, row_width), BF16),
            block,
            jax.ShapeDtypeStruct((WIDTH, WIDTH), F32),
        ),
        in_specs=[SMEM, VMEM, VMEM, SMEM, VMEM, VMEM, VMEM],
        out_specs=(HBM, VMEM, VMEM),
        scratch_shapes=[
            pltpu.VMEM((tiles_dev, TILE + STAT_ROWS, row_width), BF16),
            pltpu.VMEM((seq_count, chunk + TILE + STAT_ROWS, row_width), BF16),
            pltpu.SemaphoreType.DMA((seq_count,)),
        ],
        compiler_params=PARAMS,
        name="forward",
    )(table, fetched, queries, core, grad_t, other_t, grads)
    arrived = exchange(second)

    run = grad_mixed.shape[1]
    blocks = model // run // 2
    shares = jax.ShapeDtypeStruct((blocks, run, tok_rows), BF16)
    mine, sent = pl.pallas_call(
        mixed_kernel,
        out_shape=(shares, shares),
        in_specs=[SMEM, HBM, VMEM],
        out_specs=(VMEM, VMEM),
        scratch_shapes=[pltpu.VMEM(out_weight.shape, BF16), pltpu.SemaphoreType.DMA],
        compiler_params=PARAMS,
        name="mixed_share",
    )(core, stay(out_weight), attention)
    mine, next_1, back_1, next_2, back_2 = pl.pallas_call(
        pair_kernel,
        out_shape=(
            jax.ShapeDtypeStruct((2, run, tok_rows), F32),
            jax.ShapeDtypeStruct((2, run, tok_rows), BF16),
            jax.ShapeDtypeStruct((2, run, tok_rows), BF16),
            jax.ShapeDtypeStruct((1, run, tok_rows), BF16),
            jax.ShapeDtypeStruct((1, run, tok_rows), BF16),
        ),
        in_specs=[SMEM, VMEM, VMEM],
        out_specs=(VMEM,) * 5,
        compiler_params=PARAMS,
        name="mixed_pair",
    )(lax.axis_index("z")[None].astype(jnp.int32), mine, swap_cores(sent))
    mine, sent = pl.pallas_call(
        near_kernel,
        out_shape=(
            jax.ShapeDtypeStruct((run, tok_rows), F32),
            jax.ShapeDtypeStruct((run, tok_rows), BF16),
        ),
        in_specs=[VMEM] * 4,
        out_specs=(VMEM, VMEM),
        compiler_params=PARAMS,
        name="mixed_near",
    )(mine, to_chip(next_1, 1), to_chip(back_1, -1), to_chip(next_2, 2))

    grad_queries, requests = pl.pallas_call(
        functools.partial(query_kernel, scale, list_length),
        out_shape=(block, pltpu.HBM((seq_count, TILE, row_width), BF16)),
        in_specs=[SMEM, VMEM, VMEM, VMEM, VMEM],
        out_specs=(VMEM, HBM),
        scratch_shapes=[pltpu.SemaphoreType.DMA],
        compiler_params=PARAMS,
        cost_estimate=pl.CostEstimate(flops=400_000_000, bytes_accessed=4_000_000, transcendentals=300_000),
        name="query_grad",
    )(table, fetched, queries, grads, stats)

    third = pl.pallas_call(
        functools.partial(sum_kernel, chunk),
        out_shape=pltpu.HBM((seq_count, chunk, row_width), BF16),
        in_specs=[VMEM, ANY, HBM],
        out_specs=HBM,
        scratch_shapes=[pltpu.VMEM((4, chunk, row_width), BF16), pltpu.SemaphoreType.DMA((seq_count // 4,))],
        compiler_params=PARAMS,
        name="sum_share",
    )(arrived, sent, stay(grad_queries))
    gathered = exchange(third)

    grad_keys, grad_values = pl.pallas_call(
        functools.partial(owner_kernel, scale, chunk, 4),
        out_shape=(block, block),
        in_specs=[SMEM, HBM, VMEM, VMEM, VMEM],
        out_specs=(VMEM, VMEM),
        scratch_shapes=[
            pltpu.VMEM((tok_rows, row_width), F32),
            pltpu.VMEM((tok_rows, row_width), F32),
            pltpu.VMEM((seq_count, TILE, row_width), BF16),
            pltpu.SemaphoreType.DMA((seq_count // 4,)),
        ],
        compiler_params=PARAMS,
        cost_estimate=pl.CostEstimate(flops=1_100_000_000, bytes_accessed=4_000_000, transcendentals=1_000_000),
        name="owner_grad",
    )(table, stay(requests), arrived, keys, values)
    mixed = pl.pallas_call(
        last_kernel,
        out_shape=jax.ShapeDtypeStruct((run, tok_rows), BF16),
        in_specs=[VMEM, VMEM, VMEM, HBM],
        out_specs=VMEM,
        compiler_params=PARAMS,
        name="mixed_last",
    )(mine, to_chip(back_2, -2), to_chip(sent, 4), stay(grad_keys)).T
    written = pl.pallas_call(
        write_kernel,
        out_shape=pltpu.HBM(gathered.shape, BF16),
        in_specs=[VMEM],
        out_specs=HBM,
        scratch_shapes=[pltpu.SemaphoreType.DMA],
        compiler_params=PARAMS,
        name="write",
    )(pltpu.with_memory_space_constraint(gathered, pltpu.VMEM))
    weight_grad = (
        written.reshape(row_width // FEW, seq_count * FEW // row_width, chunk // FEW, FEW, WIDTH)
        .transpose(0, 3, 1, 2, 4)
        .reshape(out_weight.shape)
    )
    return (mixed, grad_queries, grad_keys, grad_values, weight_grad)


def solution(mesh):
    seq_count, head_count = mesh.devices.shape
    split = Mesh(mesh.devices.reshape(seq_count, head_count // 2, 2), ("seq", "z", "core"))
    both = P("seq", ("z", "core"))
    rows = P(("z", "core"), None)
    return jax.shard_map(
        body,
        mesh=split,
        in_specs=(both, both, both, rows, both, P(), P()),
        out_specs=(both, both, both, both, rows),
        check_vma=False,
    )
```
